32 devices in a mesh: cells: 8 (over z, x), chan: 4 (over y, core).
Axes of the slice: x: 2, y: 2, z: 4, core: 2. Of those that a mesh axis runs over, the one named last changes fastest.
Arguments:
- charges: bfloat16 [128, 8192], P('chan', 'cells'), may hold values from -6 to 6
- basis: float32 [25, 8192], P(None, 'cells'), may hold values from -1.5 to 1.5
- atom_leaf: int32 [8192], P('cells'), may hold values from 0 to 1023, as said below
- leaf_lists: int32 [64, 1024], P(None, 'cells'), may hold values from -1 to 1023, as said below
- coarse_lists: int32 [64, 128], P(None, 'cells'), may hold values from -1 to 127, as said below
- up_ops: bfloat16 [8, 25, 25], replicated, may hold values from -0.4375 to 0.4375
- down_ops: bfloat16 [8, 25, 25], replicated, may hold values from -1.25 to 1.25
- leaf_ops: bfloat16 [25, 25, 64], replicated, may hold values from -0.15625 to 0.15625
- coarse_ops: bfloat16 [25, 25, 64], replicated, may hold values from -0.15625 to 0.15625
- mix: bfloat16 [128, 128], replicated, may hold values from -0.5 to 0.5
- cotangent: bfloat16 [128, 8192], P('chan', 'cells'), may hold values from -0.016479492 to 0.016479492
Outputs:
- refined: bfloat16 [128, 8192], P('chan', 'cells')
- grad_leaf_ops: float32 [25, 25, 64], replicated
- grad_coarse_ops: float32 [25, 25, 64], replicated
The draws below stay inside these ranges and needn't reach their ends.
Inputs may be any that keep to these rules, and one draw needn't show every extreme that they name: `atom_leaf`: an atom's leaf is one of the 128 consecutive leaves whose block along cells holds that atom. `leaf_lists`: entry [s, t] is -1 for an empty slot, else a leaf within 64 leaves of the block of 128 leaves that holds t. `coarse_lists`: entry [s, p] is -1 for an empty slot, else a parent cell within 8 cells of the block of 16 parent cells that holds p.
All inputs are finite; a program needn't handle non-finite values.
Results may differ from the reference program's by a relative error of at most 0.014.
Values may be sent and summed in bfloat16 or wider, within the bound.
No kernel may reach another device: no remote copies, remote signals or barrier semaphores. Data moves between devices by JAX's collectives and lax.ppermute only.
A program may use at most 128 MiB of HBM per device.

```python
import jax
import jax.numpy as jnp
from jax import lax

C = 128
K = 25
SLOTS = 64
LEAF_DEV = 128
ATOMS_DEV = 1024
LEAVES = 1024
COARSE = 128
ATOMS = 8192


def neighbour_lists(key, per_device, reach, overall):
    target = jnp.arange(overall, dtype=jnp.int32)[None, :]
    local_cell = target % per_device
    offset_cells = jax.random.randint(jax.random.fold_in(key, 11), (SLOTS, overall), -reach, reach + 1, dtype=jnp.int32)
    slot_index = jnp.arange(SLOTS, dtype=jnp.int32)[:, None]
    low_edge = (slot_index == 0) & (local_cell == 0)
    high_edge = (slot_index == 1) & (local_cell == per_device - 1)
    offset_cells = jnp.where(low_edge, -reach, jnp.where(high_edge, reach, offset_cells))
    partner = target + offset_cells
    dropped = jax.random.randint(jax.random.fold_in(key, 12), (SLOTS, overall), 0, 5, dtype=jnp.int32) == 0
    vacant = (dropped | (offset_cells == 0)) & jnp.logical_not(low_edge | high_edge)
    vacant = vacant | (partner < 0) | (partner >= overall)
    return jnp.where(vacant, -1, partner).astype(jnp.int32)


def draw_leaf_lists(key, part):
    return neighbour_lists(key, LEAF_DEV, LEAF_DEV // 2, LEAVES)


def draw_coarse_lists(key, part):
    return neighbour_lists(jax.random.fold_in(key, 5), LEAF_DEV // 8, LEAF_DEV // 16, COARSE)


def draw_atom_leaf(key, part):
    atom_index = jnp.arange(ATOMS, dtype=jnp.int32)
    device_of = atom_index // ATOMS_DEV
    within = atom_index % ATOMS_DEV
    first_draw = jax.random.randint(jax.random.fold_in(key, 21), (ATOMS,), 0, LEAF_DEV, dtype=jnp.int32)
    second_draw = jax.random.randint(jax.random.fold_in(key, 22), (ATOMS,), 1, LEAF_DEV + 1, dtype=jnp.int32)
    leaf_cell = first_draw * second_draw // LEAF_DEV
    leaf_cell = jnp.where(within == 0, LEAF_DEV - 1, jnp.where(within == 1, 0, leaf_cell))
    return (device_of * LEAF_DEV + leaf_cell).astype(jnp.int32)


def level_of(own_key, extent, split, low, largest):
    factor_of = 1.0
    for axis_at, blocks in split:
        steps = jax.random.uniform(jax.random.fold_in(jax.random.fold_in(own_key, 6), axis_at), (blocks,), jnp.float32, low / len(split), largest / len(split))
        factor_of = factor_of * jnp.repeat(jnp.exp(steps), extent[axis_at] // blocks).reshape((-1,) + (1,) * (len(extent) - 1 - axis_at))
    return factor_of


def centred(key, dims, deviation, most, cuts=(), kind=jnp.bfloat16):
    loudness = level_of(key, dims, cuts, -0.22, 0.18) if cuts else 1.0
    array = jax.random.normal(key, dims, jnp.float32) * deviation * loudness
    return jnp.minimum(jnp.maximum(array, -most), most).astype(kind)


def setup_inputs(seed: int = 0) -> dict:
    arg_keys = jax.random.split(jax.random.key(seed), 12)
    return {
        "charges": centred(arg_keys[0], (C, ATOMS), 1.0, 6.0, ((0, 4), (1, 8))),
        "basis": centred(arg_keys[1], (K, ATOMS), 0.25, 1.5, ((1, 8),), jnp.float32),
        "atom_leaf": draw_atom_leaf(jax.random.fold_in(arg_keys[11], 71), 0),
        "leaf_lists": draw_leaf_lists(jax.random.fold_in(arg_keys[11], 71), 0),
        "coarse_lists": draw_coarse_lists(jax.random.fold_in(arg_keys[11], 71), 0),
        "up_ops": centred(arg_keys[5], (8, K, K), (8 * K) ** -0.5, 0.4375),
        "down_ops": centred(arg_keys[6], (8, K, K), K ** -0.5, 1.25),
        "leaf_ops": centred(arg_keys[7], (K, K, SLOTS), (K * SLOTS) ** -0.5, 0.15625),
        "coarse_ops": centred(arg_keys[8], (K, K, SLOTS), (K * SLOTS) ** -0.5, 0.15625),
        "mix": centred(arg_keys[9], (C, C), C ** -0.5, 0.5),
        "cotangent": centred(arg_keys[10], (C, ATOMS), ((C * LEAVES) ** -0.5), 0.016479492, ((0, 4), (1, 8))),
    }


def to_leaves(weights, values, atom_leaf):
    def one_row(row):
        scaled = (row[None, :] * values).astype(jnp.bfloat16)
        scaled = lax.optimization_barrier(scaled).astype(jnp.float32)
        return jax.ops.segment_sum(scaled.T, atom_leaf, num_segments=LEAVES).T
    return lax.map(one_row, weights)


def from_leaves(weights, fields, atom_leaf):
    def advance(running, pieces):
        row, field = pieces
        return running + row[None, :] * jnp.take(field.astype(jnp.float32), atom_leaf, axis=1), None
    start_value = jnp.zeros((fields.shape[1], weights.shape[1]), jnp.float32)
    running, _ = lax.scan(advance, start_value, (weights, fields))
    return running


def pick(multipoles, slot_list):
    valid = slot_list >= 0
    picked = jnp.take(multipoles, jnp.where(valid, slot_list, 0).astype(jnp.int32), axis=2).astype(jnp.float32)
    return picked * valid.astype(jnp.float32)[None, None, :]


def translate(multipoles, lists, ops):
    slot_first = jnp.transpose(ops, (2, 0, 1))

    def advance(running, pieces):
        slot_list, slot_op = pieces
        picked = pick(multipoles, slot_list)
        return running + jnp.einsum("kj,jct->kct", slot_op.astype(jnp.float32), picked, precision=lax.Precision.HIGHEST), None
    start_value = jnp.zeros((multipoles.shape[0], multipoles.shape[1], lists.shape[1]), jnp.float32)
    running, _ = lax.scan(advance, start_value, (lists, slot_first))
    return running


def slot_gradients(multipoles, lists, fields):
    wide = fields.astype(jnp.float32)

    def one_slot(slot_list):
        return jnp.einsum("kct,jct->kj", wide, pick(multipoles, slot_list), precision=lax.Precision.HIGHEST)
    return jnp.transpose(lax.map(one_slot, lists), (1, 2, 0))


def reference(charges, basis, atom_leaf, leaf_lists, coarse_lists, up_ops, down_ops, leaf_ops, coarse_ops, mix, cotangent):
    highest = lax.Precision.HIGHEST
    moments = to_leaves(basis, charges.astype(jnp.float32), atom_leaf).astype(jnp.bfloat16)
    grouped = moments.astype(jnp.float32).reshape(K, C, COARSE, 8)
    coarse = jnp.einsum("okj,jcpo->kcp", up_ops.astype(jnp.float32), grouped, precision=highest).astype(jnp.bfloat16)
    near_field = translate(moments, leaf_lists, leaf_ops)
    far_field = translate(coarse, coarse_lists, coarse_ops).astype(jnp.bfloat16)
    child = jnp.einsum("okj,jcp->kcpo", down_ops.astype(jnp.float32), far_field.astype(jnp.float32), precision=highest)
    expansion = (near_field + child.reshape(K, C, LEAVES)).astype(jnp.bfloat16)
    potential = from_leaves(basis, expansion, atom_leaf).astype(jnp.bfloat16)
    mixed = jnp.dot(mix.T, potential, preferred_element_type=jnp.float32)
    refined = (charges.astype(jnp.float32) + mixed).astype(jnp.bfloat16)
    back_potential = jnp.dot(mix, cotangent, preferred_element_type=jnp.float32).astype(jnp.bfloat16)
    back_expansion = to_leaves(basis, back_potential.astype(jnp.float32), atom_leaf).astype(jnp.bfloat16)
    back_grouped = back_expansion.astype(jnp.float32).reshape(K, C, COARSE, 8)
    back_far = jnp.einsum("okj,kcpo->jcp", down_ops.astype(jnp.float32), back_grouped, precision=highest).astype(jnp.bfloat16)
    grad_leaf_ops = slot_gradients(moments, leaf_lists, back_expansion)
    grad_coarse_ops = slot_gradients(coarse, coarse_lists, back_far)
    return refined, grad_leaf_ops, grad_coarse_ops
```

```python
import jax
import jax.numpy as jnp
from jax import lax
from jax.experimental import pallas as pl
from jax.experimental.pallas import tpu as pltpu
from jax.sharding import PartitionSpec as P

KP = 32
GROUP = 8
OCT = 8
VMEM_BYTES = 48 * 1024 * 1024
f32 = jnp.float32
bf16 = jnp.bfloat16


def nt(a, b):
    return lax.dot_general(a, b, (((1,), (1,)), ((), ())), preferred_element_type=f32)


def nn(a, b):
    return jnp.dot(a, b, preferred_element_type=f32)


def member(leaf_row, leaf_dev):
    shape = (leaf_dev, leaf_row.shape[1])
    return jnp.where(lax.broadcasted_iota(jnp.int32, shape, 0) == leaf_row, 1.0, 0.0).astype(bf16)


def padded_basis(basis_ref, base):
    base[...] = jnp.zeros_like(base)
    base[0 : basis_ref.shape[0], :] = basis_ref[...]


def spread(base, values, scaled):
    wide = values.astype(f32)
    for c in range(values.shape[0]):
        scaled[c * KP : (c + 1) * KP, :] = (base[...] * wide[c : c + 1, :]).astype(bf16)


def pooling(rows, cols):
    return jnp.where(
        lax.broadcasted_iota(jnp.int32, (rows, cols), 0) // OCT
        == lax.broadcasted_iota(jnp.int32, (rows, cols), 1),
        1.0,
        0.0,
    ).astype(bf16)


def by_octant(stacked):
    octant = lax.broadcasted_iota(jnp.int32, (KP, stacked.shape[1]), 1) % OCT
    result = stacked[0:KP, :]
    for o in range(1, OCT):
        result = jnp.where(octant == o, stacked[o * KP : (o + 1) * KP, :], result)
    return result


def upward(ops, wide_ref, store):
    lanes = OCT * 128
    pool = pooling(lanes, 128)
    for part in range(wide_ref.shape[1] // lanes):
        stacked = nn(ops, wide_ref[:, part * lanes : (part + 1) * lanes])
        store(part, nn(by_octant(stacked).astype(bf16), pool).astype(bf16))


def moments_kernel(charges, basis, leaf, m_out, hi_out, lo_out, base, scaled):
    leaf_dev = m_out.shape[1]
    half = leaf_dev // 2
    padded_basis(basis, base)
    local = leaf[...] - lax.axis_index("cells") * leaf_dev
    spread(base, charges[...], scaled)
    m = nt(scaled[...], member(local, leaf_dev))
    m_out[...] = m.astype(bf16)
    rows = m.shape[0] // 2
    first, second = m[:rows], m[rows:]
    low_lane = lax.broadcasted_iota(jnp.int32, (rows, leaf_dev), 1) < half
    hi_out[...] = jnp.where(low_lane, pltpu.roll(first, half, 1), second).astype(bf16)
    lo_out[...] = jnp.where(low_lane, first, pltpu.roll(second, half, 1)).astype(bf16)


def back_kernel(
    own, core, cross, mix, basis, leaf, m, up, down_t, be_out, bf_out, cc_out, base, scaled, gathered, wide
):
    leaf_dev = m.shape[1]
    part = own.shape[0]
    me = lax.axis_index("chan")
    padded_basis(basis, base)
    gathered[pl.ds(me * part, part), :] = own[...]
    gathered[pl.ds((me ^ 1) * part, part), :] = core[...]
    gathered[pl.ds((me ^ 2) * part, part), :] = cross[0:part, :]
    gathered[pl.ds((me ^ 3) * part, part), :] = cross[part : 2 * part, :]
    potential = nn(mix[pl.ds(me * part, part), :], gathered[...]).astype(bf16)
    local = leaf[...] - lax.axis_index("cells") * leaf_dev
    spread(base, potential, scaled)
    be = nt(scaled[...], member(local, leaf_dev)).astype(bf16)
    for c in range(part):
        be_out[:, c * leaf_dev : (c + 1) * leaf_dev] = be[c * KP : (c + 1) * KP, :]
        wide[:, c * leaf_dev : (c + 1) * leaf_dev] = m[c * KP : (c + 1) * KP, :]

    def store_far(at, value):
        bf_out[:, at * 128 : (at + 1) * 128] = value

    def store_coarse(at, value):
        cc_out[at * KP : (at + 1) * KP, :] = value

    upward(down_t[...], be_out, store_far)
    upward(up[...], wide, store_coarse)


def slot_of(group, at):
    return (at % 4) * 16 + 2 * group + at // 4


def grads_kernel(
    m, low, high, cc, ll, cl, be, bf, up, p_out, pc_out, g_out, src, srcc, idx, idxc, wide, blocks, turned
):
    step = pl.program_id(0)
    cell = lax.axis_index("cells")
    leaf_dev = m.shape[1]
    half = leaf_dev // 2
    window = 2 * leaf_dev
    channels = m.shape[0] // KP
    slots, coarse_dev = cl.shape

    @pl.when(step == 0)
    def prepare():
        src[:, 0:leaf_dev] = m[...]
        rows = low.shape[0]
        a, b = low[...].astype(f32), high[...].astype(f32)
        low_lane = lax.broadcasted_iota(jnp.int32, (rows, leaf_dev), 1) < half
        src[0:rows, leaf_dev:] = jnp.where(low_lane, a, pltpu.roll(b, half, 1)).astype(bf16)
        src[rows:, leaf_dev:] = jnp.where(low_lane, pltpu.roll(a, half, 1), b).astype(bf16)
        for c in range(channels):
            wide[:, c * leaf_dev : (c + 1) * leaf_dev] = src[c * KP : (c + 1) * KP, leaf_dev:]
        srcc[:, 0:128] = cc[...]

        def store_halo(at, value):
            srcc[at * KP : (at + 1) * KP, 128:] = value

        upward(up[...], wide, store_halo)
        rel = ll[...] - cell * leaf_dev
        place = jnp.where(rel < 0, rel + leaf_dev + half, jnp.where(rel < leaf_dev, rel, rel + half))
        idx[...] = jnp.where(ll[...] < 0, -1, place)
        crel = cl[...] - cell * coarse_dev
        side = coarse_dev // 2
        cplace = jnp.where(crel < 0, crel + 128 + side, jnp.where(crel < coarse_dev, crel, crel + 128 - side))
        cplace = jnp.where(cl[...] < 0, -1, cplace).astype(f32).astype(bf16)
        copies = jnp.where(
            lax.broadcasted_iota(jnp.int32, (coarse_dev, 128), 0)
            == lax.broadcasted_iota(jnp.int32, (coarse_dev, 128), 1) % coarse_dev,
            1.0,
            0.0,
        ).astype(bf16)
        spot = nn(cplace, copies).astype(jnp.int32)
        base = lax.broadcasted_iota(jnp.int32, (slots, 128), 1) // coarse_dev * coarse_dev
        idxc[...] = jnp.where(spot < 0, -1, spot + base)

    place_of = lax.broadcasted_iota(jnp.int32, (window, 128), 0)

    def chosen(ref, at):
        row = ref[pl.ds(slot_of(step, at), 1), :]
        return jnp.where(place_of == row, 1.0, 0.0).astype(bf16)

    for pair in range(GROUP // 2):
        at = 2 * pair
        both = jnp.concatenate([chosen(idx, at), chosen(idx, at + 1)], axis=1)
        picked = nn(src[...], both).astype(bf16)
        for i in range(2):
            for c in range(channels):
                p_out[(at + i) * KP : (at + i + 1) * KP, c * 128 : (c + 1) * 128] = picked[
                    c * KP : (c + 1) * KP, i * 128 : (i + 1) * 128
                ]
        both = jnp.concatenate([chosen(idxc, at), chosen(idxc, at + 1)], axis=1)
        picked = nn(srcc[...], both).astype(bf16)
        for i in range(2):
            for c in range(srcc.shape[0] // KP):
                pc_out[(at + i) * KP : (at + i + 1) * KP, c * 128 : (c + 1) * 128] = picked[
                    c * KP : (c + 1) * KP, i * 128 : (i + 1) * 128
                ]
    leaf_part = nt(be[...], p_out[...])
    coarse_part = nt(bf[...], pc_out[...])
    for i in range(2):
        blocks[2 * step + i] = leaf_part[:, i * 128 : (i + 1) * 128]
        blocks[slots // 4 + 2 * step + i] = coarse_part[:, i * 128 : (i + 1) * 128]

    @pl.when(step == slots // GROUP - 1)
    def finish():
        for b in range(slots // 2):
            turned[:, b, :] = blocks[b]
        g_out[...] = turned[...].astype(bf16)


def potential_kernel(p, pc, lops, cops, down, basis, leaf, out, near, far, base, field, total):
    step = pl.program_id(0)
    leaf_dev = p.shape[1] // out.shape[0]

    @pl.when(step == 0)
    def start():
        near[...] = nn(lops[...], p[...])
        far[...] = nn(cops[...], pc[...])

    @pl.when(step > 0)
    def advance():
        near[...] += nn(lops[...], p[...])
        far[...] += nn(cops[...], pc[...])

    @pl.when(step == pl.num_programs(0) - 1)
    def finish():
        padded_basis(basis, base)
        local = leaf[...] - lax.axis_index("cells") * leaf_dev
        inside = member(local, leaf_dev)
        lanes = OCT * 128
        copies = jnp.where(
            lax.broadcasted_iota(jnp.int32, (128, lanes), 1) // OCT
            == lax.broadcasted_iota(jnp.int32, (128, lanes), 0),
            1.0,
            0.0,
        ).astype(bf16)
        for part in range(far.shape[1] // 128):
            parent = nn(far[:, part * 128 : (part + 1) * 128].astype(bf16), copies).astype(bf16)
            child = by_octant(nn(down[...], parent))
            expansion = (near[:, part * lanes : (part + 1) * lanes] + child).astype(bf16)
            for c in range(OCT):
                field[c * KP : (c + 1) * KP, :] = expansion[:, c * leaf_dev : (c + 1) * leaf_dev]
            per_atom = nn(field[...], inside)
            for c in range(OCT):
                at = part * OCT + c
                total[at : at + 1, :] = jnp.sum(
                    base[...] * per_atom[c * KP : (c + 1) * KP, :], axis=0, keepdims=True
                )
        out[...] = total[...].astype(bf16)


def reduce_kernel(parts, out):
    total = parts[0].astype(f32)
    for d in range(1, parts.shape[0]):
        total = total + parts[d].astype(f32)
    turned = total.T
    pieces = []
    for level in range(2):
        for place in range(4):
            pieces.append(turned[place * KP : (place + 1) * KP, level * 16 : (level + 1) * 16])
    laid = jnp.concatenate(pieces, axis=1).astype(bf16)
    for d in range(out.shape[0]):
        out[d] = laid


def unpack_kernel(whole, leaf_out, coarse_out):
    kcount, jcount, slots = leaf_out.shape
    for k in range(kcount):
        row = whole[k].astype(f32)
        leaf_out[k] = row[0:jcount, 0:slots]
        coarse_out[k] = pltpu.roll(row, slots, 1)[0:jcount, 0:slots]


def mixing_kernel(own, core, cross, mix, charges, out, gathered, mixed):
    part = own.shape[0]
    me = lax.axis_index("chan")
    gathered[pl.ds(me * part, part), :] = own[...]
    gathered[pl.ds((me ^ 1) * part, part), :] = core[...]
    gathered[pl.ds((me ^ 2) * part, part), :] = cross[0:part, :]
    gathered[pl.ds((me ^ 3) * part, part), :] = cross[part : 2 * part, :]
    mixed[...] = lax.dot_general(
        mix[...], gathered[...], (((0,), (0,)), ((), ())), preferred_element_type=f32
    )
    out[...] = (charges[...].astype(f32) + mixed[pl.ds(me * part, part), :]).astype(bf16)


def call(kernel, outs, scratch, flops=10**8, moved=10**6, **kw):
    return pl.pallas_call(
        kernel,
        out_shape=outs,
        scratch_shapes=scratch,
        compiler_params=pltpu.CompilerParams(vmem_limit_bytes=VMEM_BYTES),
        cost_estimate=pl.CostEstimate(flops=flops, bytes_accessed=moved, transcendentals=0),
        **kw,
    )


def from_chan(block):
    count = lax.axis_size("chan")
    core = lax.ppermute(block, "chan", [(i, i ^ 1) for i in range(count)])
    cross = lax.ppermute(
        jnp.concatenate([block, core], axis=0), "chan", [(i, i ^ 2) for i in range(count)]
    )
    return core, cross


def slot_ops(ops):
    kcount, _, slots = ops.shape
    laid = jnp.transpose(ops.reshape(kcount, kcount, 4, slots // 4), (0, 3, 2, 1))
    laid = jnp.pad(laid, ((0, KP - kcount), (0, 0), (0, 0), (0, KP - kcount)))
    return laid.reshape(KP, slots * KP)


def octant_ops(ops):
    kcount = ops.shape[1]
    return jnp.pad(ops, ((0, 0), (0, KP - kcount), (0, KP - kcount))).reshape(OCT * KP, KP)


def local(
    charges, basis, atom_leaf, leaf_lists, coarse_lists, up_ops, down_ops, leaf_ops, coarse_ops, mix, cotangent
):
    part, atoms = charges.shape
    kcount = basis.shape[0]
    slots, leaf_dev = leaf_lists.shape
    rows = part * KP
    steps = slots // GROUP
    cells = lax.axis_size("cells")
    devices = cells * lax.axis_size("chan")
    leaf = atom_leaf.reshape(1, atoms)
    shape = jax.ShapeDtypeStruct

    cot_core, cot_cross = from_chan(cotangent)
    m, hi, lo = call(
        moments_kernel,
        (
            shape((rows, leaf_dev), bf16),
            shape((rows // 2, leaf_dev), bf16),
            shape((rows // 2, leaf_dev), bf16),
        ),
        [pltpu.VMEM((KP, atoms), f32), pltpu.VMEM((rows, atoms), bf16)],
    )(charges, basis, leaf)
    forward = [(i, i + 1) for i in range(cells - 1)]
    low = lax.ppermute(hi, "cells", forward)
    high = lax.ppermute(lo, "cells", [(b, a) for a, b in forward])

    up = octant_ops(up_ops)
    down_t = octant_ops(jnp.swapaxes(down_ops, 1, 2))
    down = octant_ops(down_ops)
    be, bf, cc = call(
        back_kernel,
        (
            shape((KP, part * leaf_dev), bf16),
            shape((KP, part * leaf_dev // OCT), bf16),
            shape((128, 128), bf16),
        ),
        [
            pltpu.VMEM((KP, atoms), f32),
            pltpu.VMEM((rows, atoms), bf16),
            pltpu.VMEM((mix.shape[0], atoms), bf16),
            pltpu.VMEM((KP, part * leaf_dev), bf16),
        ],
    )(cotangent, cot_core, cot_cross, mix, basis, leaf, m, up, down_t)

    full = lambda a: pl.BlockSpec(a.shape, lambda g: (0,) * a.ndim)
    wide = part * leaf_dev
    operands = (m, low, high, cc, leaf_lists, coarse_lists, be, bf, up)
    p, pc, grads = call(
        grads_kernel,
        (
            shape((slots * KP, wide), bf16),
            shape((slots * KP, wide // OCT), bf16),
            shape((KP, slots // 2, 128), bf16),
        ),
        [
            pltpu.VMEM((rows, 2 * leaf_dev), bf16),
            pltpu.VMEM((128, 256), bf16),
            pltpu.VMEM((slots, 128), jnp.int32),
            pltpu.VMEM((slots, 128), jnp.int32),
            pltpu.VMEM((KP, wide), bf16),
            pltpu.VMEM((slots // 2, KP, 128), f32),
            pltpu.VMEM((KP, slots // 2, 128), f32),
        ],
        grid=(steps,),
        in_specs=[full(a) for a in operands],
        out_specs=[
            pl.BlockSpec((GROUP * KP, wide), lambda g: (g, 0)),
            pl.BlockSpec((GROUP * KP, wide // OCT), lambda g: (g, 0)),
            pl.BlockSpec((KP, slots // 2, 128), lambda g: (0, 0, 0)),
        ],
    )(*operands)

    axes = ("cells", "chan")
    if devices == KP:
        parts = lax.all_to_all(grads, axes, 0, 0)
        spread_out = call(reduce_kernel, shape((devices, KP, 128), bf16), [])(parts)
        whole = lax.all_to_all(spread_out, axes, 0, 0)
    else:
        laid = grads.reshape(KP, 2, slots // 4, 4, KP)
        laid = jnp.transpose(laid, (0, 4, 1, 3, 2)).reshape(devices, -1, 128)
        parts = lax.all_to_all(laid, axes, 0, 0)
        mine = jnp.sum(parts.astype(f32), axis=0).astype(bf16)
        whole = lax.all_gather(mine, axes).reshape(KP, KP, 128)
    grad_shape = shape((kcount, kcount, slots), f32)
    grad_leaf, grad_coarse = call(unpack_kernel, (grad_shape, grad_shape), [])(whole)

    lops, cops = slot_ops(leaf_ops), slot_ops(coarse_ops)
    small = (down, basis, leaf)
    potential = call(
        potential_kernel,
        shape((part, atoms), bf16),
        [
            pltpu.VMEM((KP, wide), f32),
            pltpu.VMEM((KP, wide // OCT), f32),
            pltpu.VMEM((KP, atoms), f32),
            pltpu.VMEM((OCT * KP, leaf_dev), bf16),
            pltpu.VMEM((part, atoms), f32),
        ],
        grid=(steps,),
        in_specs=[
            pl.BlockSpec((GROUP * KP, wide), lambda g: (g, 0)),
            pl.BlockSpec((GROUP * KP, wide // OCT), lambda g: (g, 0)),
            pl.BlockSpec((KP, GROUP * KP), lambda g: (0, g)),
            pl.BlockSpec((KP, GROUP * KP), lambda g: (0, g)),
        ]
        + [full(a) for a in small],
        out_specs=pl.BlockSpec((part, atoms), lambda g: (0, 0)),
    )(p, pc, lops, cops, *small)
    pot_core, pot_cross = from_chan(potential)
    refined = call(
        mixing_kernel,
        shape((part, atoms), bf16),
        [pltpu.VMEM((mix.shape[0], atoms), bf16), pltpu.VMEM((mix.shape[0], atoms), f32)],
    )(potential, pot_core, pot_cross, mix, charges)
    return refined, grad_leaf, grad_coarse


def solution(mesh):
    placed = (
        P("chan", "cells"),
        P(None, "cells"),
        P("cells"),
        P(None, "cells"),
        P(None, "cells"),
        P(),
        P(),
        P(),
        P(),
        P(),
        P("chan", "cells"),
    )
    return jax.shard_map(
        local, mesh=mesh, in_specs=placed, out_specs=(P("chan", "cells"), P(), P()), check_vma=False
    )
```

```python
import jax
import jax.numpy as jnp
from jax import lax
from jax.experimental import pallas as pl
from jax.experimental.pallas import tpu as pltpu
from jax.sharding import PartitionSpec as P

KP = 32
GROUP = 8
CHUNK = 128
OCT = 8
MORE = 8
VMEM_BYTES = 24 * 1024 * 1024
f32 = jnp.float32
bf16 = jnp.bfloat16


def nt(a, b):
    return lax.dot_general(a, b, (((1,), (1,)), ((), ())), preferred_element_type=f32)


def nn(a, b):
    return jnp.dot(a, b, preferred_element_type=f32)


def member(leaf_row, leaf_dev):
    shape = (leaf_dev, leaf_row.shape[1])
    return jnp.where(lax.broadcasted_iota(jnp.int32, shape, 0) == leaf_row, 1.0, 0.0).astype(bf16)


def spread(base, values, scaled):
    wide = values.astype(f32)
    for c in range(values.shape[0]):
        scaled[c * KP : (c + 1) * KP, :] = (base[...] * wide[c : c + 1, :]).astype(bf16)


def fetch(pairs, sems):
    copies = [pltpu.make_async_copy(src, dst, sems.at[i]) for i, (src, dst) in enumerate(pairs)]
    for copy in copies:
        copy.start()
    return copies


def pooling(rows, cols):
    return jnp.where(
        lax.broadcasted_iota(jnp.int32, (rows, cols), 0) // OCT
        == lax.broadcasted_iota(jnp.int32, (rows, cols), 1),
        1.0,
        0.0,
    ).astype(bf16)


def by_octant(values):
    octant = lax.broadcasted_iota(jnp.int32, (1, values.shape[1]), 1) % OCT
    return jnp.concatenate(
        [values * jnp.where(octant == o, 1.0, 0.0).astype(values.dtype) for o in range(OCT)], axis=0
    )


def upward(ops, wide_ref, sums):
    lanes = OCT * 128
    for part in range(wide_ref.shape[1] // lanes):
        spaced = by_octant(wide_ref[:, part * lanes : (part + 1) * lanes])
        sums[part * KP : (part + 1) * KP, :] = nn(ops, spaced).astype(bf16)
    return nn(sums[...], pooling(lanes, 128)).astype(bf16)


def moments_kernel(charges_hbm, basis_hbm, leaf_hbm, *rest):
    more = rest[:MORE]
    m_out, first_out, second_out, base_out, inside_out, charges = rest[MORE : MORE + 6]
    held = rest[MORE + 6 : 2 * MORE + 6]
    basis, leaf, scaled, sems = rest[2 * MORE + 6 :]
    leaf_dev = m_out.shape[1]
    half = leaf_dev // 2
    cell = lax.axis_index("cells")
    copies = fetch(
        [(charges_hbm, charges), (basis_hbm, basis), (leaf_hbm, leaf), *zip(more, held)], sems
    )
    kcount = basis.shape[0]
    base_out[...] = jnp.zeros_like(base_out)
    for copy in copies[:3]:
        copy.wait()
    base_out[0:kcount, :] = basis[...]
    inside_out[...] = member(leaf[...] - cell * leaf_dev, leaf_dev)
    spread(base_out, charges[...], scaled)
    m = nt(scaled[...], inside_out[...])
    m_out[...] = m.astype(bf16)
    rows = m.shape[0] // 2
    upper, lower = m[:rows], m[rows:]
    low_lane = lax.broadcasted_iota(jnp.int32, (rows, leaf_dev), 1) < half
    hi = jnp.where(low_lane, pltpu.roll(upper, half, 1), lower).astype(bf16)
    lo = jnp.where(low_lane, upper, pltpu.roll(lower, half, 1)).astype(bf16)
    odd = lax.rem(cell, 2)
    first_out[...] = jnp.where(odd == 1, hi, lo)
    second_out[...] = jnp.where(odd == 1, lo, hi)
    for copy in copies[3:]:
        copy.wait()


def slot_ops(ops, padded, turned, out):
    kcount, jcount, slots = ops.shape
    turned[...] = jnp.zeros_like(turned)
    padded[...] = jnp.zeros_like(padded)
    for k in range(kcount):
        padded[k, 0:jcount, 0:slots] = ops[k].astype(f32)
        turned[k, :, :] = padded[k].T[0:slots]
    blocks = slots // 4
    for b in range(blocks):
        out[:, b * 128 : (b + 1) * 128] = jnp.concatenate(
            [turned[:, place * blocks + b, :] for place in range(4)], axis=1
        ).astype(bf16)


def prepare_kernel(
    up,
    down,
    lops,
    cops,
    ll,
    cl,
    m,
    cc_out,
    up_out,
    down_out,
    back_out,
    lops_out,
    cops_out,
    idx,
    idxc,
    wide,
    stack,
    padded,
    turned,
    sums,
):
    leaf_dev = m.shape[1]
    half = leaf_dev // 2
    kcount = up.shape[0]
    coarse_dev, slots = cl.shape
    cell = lax.axis_index("cells")
    for c in range(m.shape[0] // KP):
        wide[:, c * leaf_dev : (c + 1) * leaf_dev] = m[c * KP : (c + 1) * KP, :]
    stack[...] = jnp.zeros_like(stack)
    for k in range(kcount):
        stack[0, :, k, 0:kcount] = up[k].astype(f32)
        stack[1, :, k, 0:kcount] = down[k].astype(f32)

    def side_by_side(pieces):
        return jnp.concatenate(pieces, axis=1).astype(bf16)

    up_out[...] = side_by_side([stack[0, o, :, 0:KP] for o in range(OCT)])
    down_out[...] = side_by_side([stack[1, o, :, 0:KP] for o in range(OCT)])
    back_out[...] = side_by_side([stack[1, o].T[0:KP, :] for o in range(OCT)])
    cc_out[...] = upward(up_out[...], wide, sums)

    slot_ops(lops, padded, turned, lops_out)
    slot_ops(cops, padded, turned, cops_out)
    rel = ll[...] - cell * leaf_dev
    place = jnp.where(rel < 0, rel + leaf_dev + half, jnp.where(rel < leaf_dev, rel, rel + half))
    idx[...] = jnp.where(ll[...] < 0, -1, place)
    crel = cl[...] - cell * coarse_dev
    side = coarse_dev // 2
    cplace = jnp.where(crel < 0, crel + 128 + side, jnp.where(crel < coarse_dev, crel, crel + 128 - side))
    cplace = jnp.where(cl[...] < 0, -1, cplace).astype(f32).astype(bf16)
    copied = jnp.where(
        lax.broadcasted_iota(jnp.int32, (coarse_dev, 128), 0)
        == lax.broadcasted_iota(jnp.int32, (coarse_dev, 128), 1) % coarse_dev,
        1.0,
        0.0,
    ).astype(bf16)
    spot = lax.dot_general(cplace, copied, (((0,), (0,)), ((), ())), preferred_element_type=f32)
    spot = spot.astype(jnp.int32)
    start = lax.broadcasted_iota(jnp.int32, (slots, 128), 1) // coarse_dev * coarse_dev
    idxc[...] = jnp.where(spot < 0, -1, spot + start)


def back_kernel(own, core, cross, other, mix, base, inside, back_ops, be_out, bf_out, scaled, gathered, sums):
    leaf_dev = inside.shape[0]
    part = own.shape[0]
    me = lax.axis_index("chan")
    gathered[pl.ds(me * part, part), :] = own[...]
    gathered[pl.ds((me ^ 1) * part, part), :] = core[...]
    gathered[pl.ds((me ^ 2) * part, part), :] = cross[...]
    gathered[pl.ds((me ^ 3) * part, part), :] = other[...]
    potential = nn(mix[pl.ds(me * part, part), :], gathered[...]).astype(bf16)
    spread(base, potential, scaled)
    be = nt(scaled[...], inside[...]).astype(bf16)
    for c in range(part):
        be_out[:, c * leaf_dev : (c + 1) * leaf_dev] = be[c * KP : (c + 1) * KP, :]
    far = upward(back_ops[...], be_out, sums)
    for at in range(far.shape[0] // KP):
        bf_out[:, at * 128 : (at + 1) * 128] = far[at * KP : (at + 1) * KP, :]


def slot_of(group, at):
    return (at % 4) * 16 + 2 * group + at // 4


def grads_kernel(
    m,
    first,
    second,
    cc,
    be,
    bf,
    up,
    idx,
    idxc,
    lops,
    cops,
    near,
    far,
    g_out,
    src,
    srcc,
    wide,
    even,
    odd,
    even_c,
    odd_c,
    sums,
    blocks,
    turned,
):
    leaf_dev = m.shape[1]
    half = leaf_dev // 2
    window = 2 * leaf_dev
    channels = m.shape[0] // KP
    slots = idx.shape[0]
    steps = slots // GROUP
    rows = GROUP * KP
    is_odd = lax.rem(lax.axis_index("cells"), 2) == 1

    src[:, 0:leaf_dev] = m[...]
    mid = first.shape[0]
    a, b = first[...].astype(f32), second[...].astype(f32)
    low, high = jnp.where(is_odd, b, a), jnp.where(is_odd, a, b)
    low_lane = lax.broadcasted_iota(jnp.int32, (mid, leaf_dev), 1) < half
    src[0:mid, leaf_dev:] = jnp.where(low_lane, low, pltpu.roll(high, half, 1)).astype(bf16)
    src[mid:, leaf_dev:] = jnp.where(low_lane, pltpu.roll(low, half, 1), high).astype(bf16)
    for c in range(channels):
        wide[:, c * leaf_dev : (c + 1) * leaf_dev] = src[c * KP : (c + 1) * KP, leaf_dev:]
    srcc[:, 0:128] = cc[...]
    srcc[:, 128:] = upward(up[...], wide, sums)
    place_of = lax.broadcasted_iota(jnp.int32, (window, 128), 0)

    def chosen(ref, group, at):
        row = ref[pl.ds(slot_of(group, at), 1), :]
        return jnp.where(place_of == row, 1.0, 0.0).astype(bf16)

    def picks(source, ref, group, out, chunk):
        for pair in range(GROUP // 2):
            at = 2 * pair
            both = jnp.concatenate([chosen(ref, group, at), chosen(ref, group, at + 1)], axis=1)
            for begin in range(0, source.shape[0], chunk):
                picked = nn(source[begin : begin + chunk, :], both).astype(bf16)
                for i in range(2):
                    for c in range(chunk // KP):
                        lane = (begin // KP + c) * 128
                        out[(at + i) * KP : (at + i + 1) * KP, lane : lane + 128] = picked[
                            c * KP : (c + 1) * KP, i * 128 : (i + 1) * 128
                        ]

    def products(group, held, held_c):
        leaf_part = nt(be[...], held[...])
        coarse_part = nt(bf[...], held_c[...])
        for i in range(2):
            blocks[2 * group + i] = leaf_part[:, i * 128 : (i + 1) * 128]
            blocks[2 * group + slots // 4 + i] = coarse_part[:, i * 128 : (i + 1) * 128]
        ops = pl.ds(pl.multiple_of(group * rows, rows), rows)
        near[...] += nn(lops[:, ops], held[...])
        far[...] += nn(cops[:, ops], held_c[...])

    def pick_group(group, held, held_c):
        picks(src, idx, group, held, CHUNK)
        picks(srcc, idxc, group, held_c, 128)

    near[...] = jnp.zeros_like(near)
    far[...] = jnp.zeros_like(far)
    pick_group(0, even, even_c)

    def two_groups(i, carry):
        group = 2 * i + 1
        pick_group(group, odd, odd_c)
        products(group - 1, even, even_c)
        pick_group(group + 1, even, even_c)
        products(group, odd, odd_c)
        return carry

    lax.fori_loop(0, steps // 2 - 1, two_groups, 0)
    pick_group(steps - 1, odd, odd_c)
    products(steps - 2, even, even_c)
    products(steps - 1, odd, odd_c)
    for b in range(slots // 2):
        turned[:, b, :] = blocks[b]
    g_out[...] = turned[...].astype(bf16)


def potential_kernel(near, far, down, base, inside, out, field, total):
    leaf_dev = near.shape[1] // out.shape[0]
    lanes = OCT * 128
    copies = jnp.where(
        lax.broadcasted_iota(jnp.int32, (128, lanes), 1) // OCT
        == lax.broadcasted_iota(jnp.int32, (128, lanes), 0),
        1.0,
        0.0,
    ).astype(bf16)
    for at in range(far.shape[1] // 128):
        parent = nn(far[:, at * 128 : (at + 1) * 128].astype(bf16), copies).astype(bf16)
        child = nn(down[...], by_octant(parent))
        columns = slice(at * lanes, (at + 1) * lanes)
        expansion = (near[:, columns] + child).astype(bf16)
        for c in range(OCT):
            field[c * KP : (c + 1) * KP, :] = expansion[:, c * leaf_dev : (c + 1) * leaf_dev]
        for c in range(OCT):
            row = at * OCT + c
            per_atom = nn(field[c * KP : (c + 1) * KP, :], inside[...])
            total[row : row + 1, :] = jnp.sum(base[...] * per_atom, axis=0, keepdims=True)
    out[...] = total[...].astype(bf16)


def reduce_kernel(parts, after, out):
    total = parts[0].astype(f32)
    for d in range(1, parts.shape[0]):
        total = total + parts[d].astype(f32)
    turned = total.T
    pieces = []
    for level in range(2):
        for place in range(4):
            pieces.append(turned[place * KP : (place + 1) * KP, level * 16 : (level + 1) * 16])
    laid = jnp.concatenate(pieces, axis=1).astype(bf16)
    for d in range(out.shape[0]):
        out[d] = laid


def unpack_kernel(whole, leaf_out, coarse_out):
    kcount, jcount, slots = leaf_out.shape
    for k in range(kcount):
        row = whole[k].astype(f32)
        leaf_out[k] = row[0:jcount, 0:slots]
        coarse_out[k] = pltpu.roll(row, slots, 1)[0:jcount, 0:slots]


def mixing_kernel(whole, mix, charges, out, mixed):
    part = out.shape[0]
    me = lax.axis_index("chan")
    mixed[...] = lax.dot_general(
        mix[...], whole[...], (((0,), (0,)), ((), ())), preferred_element_type=f32
    )
    out[...] = (charges[...].astype(f32) + mixed[pl.ds(me * part, part), :]).astype(bf16)


def call(kernel, outs, scratch, flops=10**8, moved=10**6, limit=VMEM_BYTES, **kw):
    return pl.pallas_call(
        kernel,
        out_shape=outs,
        scratch_shapes=scratch,
        compiler_params=pltpu.CompilerParams(vmem_limit_bytes=limit),
        cost_estimate=pl.CostEstimate(flops=flops, bytes_accessed=moved, transcendentals=0),
        **kw,
    )


def from_chan(block):
    count = lax.axis_size("chan")
    return [lax.ppermute(block, "chan", [(i, i ^ d) for i in range(count)]) for d in range(1, count)]


def local(
    charges, basis, atom_leaf, leaf_lists, coarse_lists, up_ops, down_ops, leaf_ops, coarse_ops, mix, cotangent
):
    part, atoms = charges.shape
    kcount = basis.shape[0]
    slots, leaf_dev = leaf_lists.shape
    rows = part * KP
    steps = slots // GROUP
    cells = lax.axis_size("cells")
    devices = cells * lax.axis_size("chan")
    leaf = atom_leaf.reshape(1, atoms)
    shape = jax.ShapeDtypeStruct
    far_off = pl.BlockSpec(memory_space=pltpu.HBM)
    near_by = pl.BlockSpec(memory_space=pltpu.VMEM)
    like = lambda a: pltpu.VMEM(a.shape, a.dtype)
    stay = lambda *arrays: [pltpu.with_memory_space_constraint(a, pltpu.HBM) for a in arrays]
    wide = part * leaf_dev
    count = slots * KP

    cot = from_chan(cotangent)
    held = (
        cotangent,
        mix,
        jnp.swapaxes(up_ops, 0, 1),
        jnp.swapaxes(down_ops, 0, 1),
        leaf_ops,
        coarse_ops,
        leaf_lists,
        coarse_lists.T,
    )
    m, first, second, base, inside, charges_near, *held = call(
        moments_kernel,
        (
            shape((rows, leaf_dev), bf16),
            shape((rows // 2, leaf_dev), bf16),
            shape((rows // 2, leaf_dev), bf16),
            shape((KP, atoms), f32),
            shape((leaf_dev, atoms), bf16),
            shape(charges.shape, bf16),
            *[shape(a.shape, a.dtype) for a in held],
        ),
        [like(basis), like(leaf), pltpu.VMEM((rows, atoms), bf16), pltpu.SemaphoreType.DMA((3 + MORE,))],
        in_specs=[far_off] * (3 + MORE),
    )(*stay(charges, basis, leaf, *held))
    inner = [(i, i + 1) for i in range(1, cells - 1, 2)]
    outer = [(i, i + 1) for i in range(0, cells - 1, 2)]
    first = lax.ppermute(first, "cells", inner + [(b, a) for a, b in inner])
    second = lax.ppermute(second, "cells", outer + [(b, a) for a, b in outer])
    own, mix_near, *prepared = held

    wide_ops = shape((KP, OCT * KP), bf16)
    cc, up, down, back_ops, lops, cops, idx, idxc = call(
        prepare_kernel,
        (
            shape((128, 128), bf16),
            wide_ops,
            wide_ops,
            wide_ops,
            shape((KP, count), bf16),
            shape((KP, count), bf16),
            shape((slots, 128), jnp.int32),
            shape((slots, 128), jnp.int32),
        ),
        [
            pltpu.VMEM((KP, wide), bf16),
            pltpu.VMEM((2, OCT, KP, 128), f32),
            pltpu.VMEM((kcount, KP, 128), f32),
            pltpu.VMEM((KP, slots, KP), f32),
            pltpu.VMEM((128, OCT * 128), bf16),
        ],
    )(*prepared, m)
    be, bf = call(
        back_kernel,
        (shape((KP, wide), bf16), shape((KP, wide // OCT), bf16)),
        [
            pltpu.VMEM((rows, atoms), bf16),
            pltpu.VMEM((mix.shape[0], atoms), bf16),
            pltpu.VMEM((128, OCT * 128), bf16),
        ],
    )(own, *cot, mix_near, base, inside, back_ops)

    near, far, grads = call(
        grads_kernel,
        (shape((KP, wide), f32), shape((KP, wide // OCT), f32), shape((KP, slots // 2, 128), bf16)),
        [
            pltpu.VMEM((rows, 2 * leaf_dev), bf16),
            pltpu.VMEM((128, 256), bf16),
            pltpu.VMEM((KP, wide), bf16),
            pltpu.VMEM((GROUP * KP, wide), bf16),
            pltpu.VMEM((GROUP * KP, wide), bf16),
            pltpu.VMEM((GROUP * KP, wide // OCT), bf16),
            pltpu.VMEM((GROUP * KP, wide // OCT), bf16),
            pltpu.VMEM((128, OCT * 128), bf16),
            pltpu.VMEM((slots // 2, KP, 128), f32),
            pltpu.VMEM((KP, slots // 2, 128), f32),
        ],
    )(m, first, second, cc, be, bf, up, idx, idxc, lops, cops)
    potential = call(
        potential_kernel,
        shape((part, atoms), bf16),
        [pltpu.VMEM((OCT * KP, leaf_dev), bf16), pltpu.VMEM((part, atoms), f32)],
    )(near, far, down, base, inside)

    axes = ("cells", "chan")
    if devices == KP:
        parts = lax.all_to_all(grads, axes, 0, 0)
        spread_out = call(
            reduce_kernel, shape((devices, KP, 128), bf16), [], in_specs=[near_by, pl.BlockSpec(memory_space=pl.ANY)]
        )(parts, potential)
        whole = lax.all_to_all(spread_out, axes, 0, 0)
    else:
        laid = grads.reshape(KP, 2, slots // 4, 4, KP)
        laid = jnp.transpose(laid, (0, 4, 1, 3, 2)).reshape(devices, -1, 128)
        parts = lax.all_to_all(laid, axes, 0, 0)
        mine = jnp.sum(parts.astype(f32), axis=0).astype(bf16)
        whole = lax.all_gather(mine, axes).reshape(KP, KP, 128)
    grad_shape = shape((kcount, kcount, slots), f32)
    grad_leaf, grad_coarse = call(unpack_kernel, (grad_shape, grad_shape), [])(whole)

    refined = call(
        mixing_kernel,
        shape((part, atoms), bf16),
        [pltpu.VMEM((mix.shape[0], atoms), f32)],
    )(lax.all_gather(potential, "chan", axis=0, tiled=True), mix_near, charges_near)
    return refined, grad_leaf, grad_coarse


def solution(mesh):
    placed = (
        P("chan", "cells"),
        P(None, "cells"),
        P("cells"),
        P(None, "cells"),
        P(None, "cells"),
        P(),
        P(),
        P(),
        P(),
        P(),
        P("chan", "cells"),
    )
    return jax.shard_map(
        local, mesh=mesh, in_specs=placed, out_specs=(P("chan", "cells"), P(), P()), check_vma=False
    )
```

```python
import functools

import jax
import jax.numpy as jnp
from jax import lax
from jax.experimental import pallas as pl
from jax.experimental.pallas import tpu as pltpu
from jax.sharding import PartitionSpec as P

KP = 32
GROUP = 8
KM = 24
CHUNK = 8
FOUR = 4
OCT = 8
MORE = 8
VMEM_BYTES = 24 * 1024 * 1024
f32 = jnp.float32
bf16 = jnp.bfloat16


def nt(a, b):
    return lax.dot_general(a, b, (((1,), (1,)), ((), ())), preferred_element_type=f32)


def nn(a, b):
    return jnp.dot(a, b, preferred_element_type=f32)


def member(leaf_row, leaf_dev):
    shape = (leaf_dev, leaf_row.shape[1])
    return jnp.where(lax.broadcasted_iota(jnp.int32, shape, 0) == leaf_row, 1.0, 0.0).astype(bf16)


def spread(base, values, scaled):
    wide = values.astype(f32)
    count = values.shape[0]
    for c in range(0, count, 2):
        pair = [base[0:KM, :] * wide[c + i : c + i + 1, :] for i in range(2)]
        scaled[c * KM : (c + 2) * KM, :] = jnp.concatenate(pair, axis=0).astype(bf16)
    scaled[count * KM :, :] = (base[KM : KM + 1, :] * wide).astype(bf16)


def lay_wide(rows, out):
    count = rows.shape[0] // (KM + 1)
    lanes = rows.shape[1]
    top = lax.broadcasted_iota(jnp.int32, (KP - KM, lanes), 0) == 0
    for c in range(count):
        last = jnp.where(top, rows[count * KM + c : count * KM + c + 1, :], 0.0)
        block = jnp.concatenate([rows[c * KM : (c + 1) * KM, :], last], axis=0)
        out[:, c * lanes : (c + 1) * lanes] = block.astype(bf16)


def fetch(pairs, sems):
    copies = [pltpu.make_async_copy(src, dst, sems.at[i]) for i, (src, dst) in enumerate(pairs)]
    for copy in copies:
        copy.start()
    return copies


def pooling(rows, cols):
    return jnp.where(
        lax.broadcasted_iota(jnp.int32, (rows, cols), 0) // OCT
        == lax.broadcasted_iota(jnp.int32, (rows, cols), 1),
        1.0,
        0.0,
    ).astype(bf16)


def by_octant(values):
    octant = lax.broadcasted_iota(jnp.int32, (1, values.shape[1]), 1) % OCT
    return jnp.concatenate(
        [values * jnp.where(octant == o, 1.0, 0.0).astype(values.dtype) for o in range(OCT)], axis=0
    )


def upward(ops, wide_ref, sums):
    lanes = OCT * 128
    for part in range(wide_ref.shape[1] // lanes):
        spaced = by_octant(wide_ref[:, part * lanes : (part + 1) * lanes])
        sums[part * KP : (part + 1) * KP, :] = nn(ops, spaced).astype(bf16)
    return nn(sums[...], pooling(lanes, 128))


def tightened(rows):
    count = rows.shape[0] // KP
    whole = [rows[c * KP : c * KP + KM] for c in range(count)]
    last = [rows[c * KP + KM : c * KP + KM + 1] for c in range(count)]
    return jnp.concatenate(whole + last, axis=0).astype(bf16)


def moments_kernel(charges_hbm, basis_hbm, leaf_hbm, *rest):
    more = rest[:MORE]
    m_out, first_out, second_out, base_out, inside_out, charges = rest[MORE : MORE + 6]
    held = rest[MORE + 6 : 2 * MORE + 6]
    basis, leaf, scaled, sems = rest[2 * MORE + 6 :]
    leaf_dev = m_out.shape[1]
    half = leaf_dev // 2
    cell = lax.axis_index("cells")
    copies = fetch(
        [(charges_hbm, charges), (basis_hbm, basis), (leaf_hbm, leaf), *zip(more, held)], sems
    )
    kcount = basis.shape[0]
    base_out[...] = jnp.zeros_like(base_out)
    for copy in copies[:3]:
        copy.wait()
    base_out[0:kcount, :] = basis[...]
    inside_out[...] = member(leaf[...] - cell * leaf_dev, leaf_dev)
    spread(base_out, charges[...], scaled)
    m = nt(scaled[...], inside_out[...])
    m_out[...] = m.astype(bf16)
    rows = m.shape[0] // 2
    upper, lower = m[:rows], m[rows:]
    low_lane = lax.broadcasted_iota(jnp.int32, (rows, leaf_dev), 1) < half
    hi = jnp.where(low_lane, pltpu.roll(upper, half, 1), lower).astype(bf16)
    lo = jnp.where(low_lane, upper, pltpu.roll(lower, half, 1)).astype(bf16)
    odd = lax.rem(cell, 2)
    first_out[...] = jnp.where(odd == 1, hi, lo)
    second_out[...] = jnp.where(odd == 1, lo, hi)
    for copy in copies[3:]:
        copy.wait()


def slot_of(group, at):
    return at * GROUP + group


def slot_ops(ops, padded, turned, out):
    kcount, jcount, slots = ops.shape
    turned[...] = jnp.zeros_like(turned)
    padded[...] = jnp.zeros_like(padded)
    for k in range(kcount):
        padded[k, 0:jcount, 0:slots] = ops[k].astype(f32)
        turned[k, :, :] = padded[k].T[0:slots]
    for group in range(out.shape[0]):
        held = [turned[:, slot_of(group, at), :] for at in range(GROUP)]
        pieces = [a[:, 0:KM] for a in held] + [a[:, KM : KM + 1] for a in held]
        pieces.append(jnp.zeros((KP, GROUP * KP - GROUP * (KM + 1)), f32))
        out[group] = jnp.concatenate(pieces, axis=1).astype(bf16)


def prepare_kernel(
    up,
    down,
    lops,
    cops,
    ll,
    cl,
    m,
    cc_out,
    up_out,
    down_out,
    back_out,
    lops_out,
    cops_out,
    idx,
    idxc,
    wide,
    stack,
    padded,
    turned,
    sums,
):
    leaf_dev = m.shape[1]
    half = leaf_dev // 2
    kcount = up.shape[0]
    coarse_dev, slots = cl.shape
    cell = lax.axis_index("cells")
    lay_wide(m[...].astype(f32), wide)
    stack[...] = jnp.zeros_like(stack)
    for k in range(kcount):
        stack[0, :, k, 0:kcount] = up[k].astype(f32)
        stack[1, :, k, 0:kcount] = down[k].astype(f32)

    def side_by_side(pieces):
        return jnp.concatenate(pieces, axis=1).astype(bf16)

    up_out[...] = side_by_side([stack[0, o, :, 0:KP] for o in range(OCT)])
    down_out[...] = side_by_side([stack[1, o, :, 0:KP] for o in range(OCT)])
    back_out[...] = side_by_side([stack[1, o].T[0:KP, :] for o in range(OCT)])
    cc_out[...] = tightened(upward(up_out[...], wide, sums))

    slot_ops(lops, padded, turned, lops_out)
    slot_ops(cops, padded, turned, cops_out)
    rel = ll[...] - cell * leaf_dev
    place = jnp.where(rel < 0, rel + leaf_dev + half, jnp.where(rel < leaf_dev, rel, rel + half))
    idx[...] = jnp.where(ll[...] < 0, -1, place)
    crel = cl[...] - cell * coarse_dev
    side = coarse_dev // 2
    cplace = jnp.where(crel < 0, crel + 128 + side, jnp.where(crel < coarse_dev, crel, crel + 128 - side))
    cplace = jnp.where(cl[...] < 0, -1, cplace).astype(f32).astype(bf16)
    copied = jnp.where(
        lax.broadcasted_iota(jnp.int32, (coarse_dev, 128), 0)
        == lax.broadcasted_iota(jnp.int32, (coarse_dev, 128), 1) % coarse_dev,
        1.0,
        0.0,
    ).astype(bf16)
    spot = lax.dot_general(cplace, copied, (((0,), (0,)), ((), ())), preferred_element_type=f32)
    spot = spot.astype(jnp.int32)
    start = lax.broadcasted_iota(jnp.int32, (slots, 128), 1) // coarse_dev * coarse_dev
    idxc[...] = jnp.where(spot < 0, -1, spot + start)


def back_kernel(own, core, cross, other, mix, base, inside, back_ops, be_out, bf_out, scaled, gathered, sums):
    part = own.shape[0]
    me = lax.axis_index("chan")
    gathered[pl.ds(me * part, part), :] = own[...]
    gathered[pl.ds((me ^ 1) * part, part), :] = core[...]
    gathered[pl.ds((me ^ 2) * part, part), :] = cross[...]
    gathered[pl.ds((me ^ 3) * part, part), :] = other[...]
    potential = nn(mix[pl.ds(me * part, part), :], gathered[...]).astype(bf16)
    spread(base, potential, scaled)
    lay_wide(nt(scaled[...], inside[...]), be_out)
    far = upward(back_ops[...], be_out, sums).astype(bf16)
    for at in range(far.shape[0] // KP):
        bf_out[:, at * 128 : (at + 1) * 128] = far[at * KP : (at + 1) * KP, :]


def grads_kernel(
    m,
    first,
    second,
    cc,
    be,
    bf,
    up,
    idx,
    idxc,
    lops,
    cops,
    near,
    far,
    g_out,
    src,
    srcc,
    wide,
    even,
    odd,
    even_c,
    odd_c,
    even_last,
    odd_last,
    even_c_last,
    odd_c_last,
    sums,
    blocks,
    flat,
    *,
    kcount,
):
    leaf_dev = m.shape[1]
    half = leaf_dev // 2
    window = 2 * leaf_dev
    channels = m.shape[0] // kcount
    steps = idx.shape[0] // GROUP
    tight = even.shape[0]
    is_odd = lax.rem(lax.axis_index("cells"), 2) == 1

    src[:, 0:leaf_dev] = m[...]
    mid = first.shape[0]
    a, b = first[...].astype(f32), second[...].astype(f32)
    low, high = jnp.where(is_odd, b, a), jnp.where(is_odd, a, b)
    low_lane = lax.broadcasted_iota(jnp.int32, (mid, leaf_dev), 1) < half
    upper = jnp.where(low_lane, low, pltpu.roll(high, half, 1))
    lower = jnp.where(low_lane, pltpu.roll(low, half, 1), high)
    src[0:mid, leaf_dev:] = upper.astype(bf16)
    src[mid:, leaf_dev:] = lower.astype(bf16)
    lay_wide(src[:, leaf_dev:].astype(f32), wide)
    srcc[:, 0:128] = cc[...]
    srcc[:, 128:] = tightened(upward(up[...], wide, sums))
    place_of = lax.broadcasted_iota(jnp.int32, (window, 128), 0)

    def chosen(ref, group, at):
        row = ref[pl.ds(slot_of(group, at), 1), :]
        return jnp.where(place_of == row, 1.0, 0.0).astype(bf16)

    def picks(source, ref, group, held, last, chunk):
        count = source.shape[0] // kcount
        for pair in range(GROUP // 2):
            at = 2 * pair
            both = jnp.concatenate([chosen(ref, group, at), chosen(ref, group, at + 1)], axis=1)
            for begin in range(0, count, chunk):
                picked = nn(source[begin * KM : (begin + chunk) * KM, :], both)
                for c in range(chunk):
                    rows = picked[c * KM : (c + 1) * KM]
                    lane = (begin + c) * 128
                    held[at * KM : (at + 2) * KM, lane : lane + 128] = jnp.concatenate(
                        [rows[:, 0:128], rows[:, 128:]], axis=0
                    ).astype(bf16)
            picked = nn(source[count * KM :, :], both)
            for i in range(2):
                for c in range(count):
                    last[at + i : at + i + 1, c * 128 : (c + 1) * 128] = picked[
                        c : c + 1, i * 128 : (i + 1) * 128
                    ]
        held[GROUP * KM :, :] = last[...].astype(bf16)

    def pick_group(group, held, last, held_c, last_c):
        picks(src, idx, group, held, last, CHUNK)
        picks(srcc, idxc, group, held_c, last_c, srcc.shape[0] // kcount)

    def products(group, held, held_c):
        blocks[group, :, 0:tight] = nt(be[...], held[...])
        blocks[steps + group, :, 0:tight] = nt(bf[...], held_c[...])
        near[...] += nn(lops[group][:, 0:tight], held[...])
        far[...] += nn(cops[group][:, 0:tight], held_c[...])

    for ref in (near, far, even_last, odd_last, even_c_last, odd_c_last):
        ref[...] = jnp.zeros_like(ref)
    evens, odds = (even, even_last, even_c, even_c_last), (odd, odd_last, odd_c, odd_c_last)
    pick_group(0, *evens)

    def two_groups(i, carry):
        group = 2 * i + 1
        pick_group(group, *odds)
        products(group - 1, even, even_c)
        pick_group(group + 1, *evens)
        products(group, odd, odd_c)
        return carry

    lax.fori_loop(0, steps // 2 - 1, two_groups, 0)
    pick_group(steps - 1, *odds)
    products(steps - 2, even, even_c)
    products(steps - 1, odd, odd_c)
    flat[...] = jnp.zeros_like(flat)
    main = GROUP * KM
    for turn in range(-(-kcount // FOUR)):
        several = jnp.concatenate([blocks[:, turn * FOUR + k, :] for k in range(FOUR)], axis=0)
        across = several.T
        for tile in range(GROUP // 2):
            at = 2 * tile
            body = jnp.concatenate([across[a * KM : (a + 1) * KM] for a in (at, at + 1)], axis=1)
            rest = jnp.concatenate([across[main + a : main + a + 1] for a in (at, at + 1)], axis=1)
            rows = pl.ds(turn * FOUR * kcount + tile, kcount, stride=FOUR)
            flat[rows, :] = jnp.concatenate([body, rest], axis=0)
    if len(g_out.shape) == 2:
        g_out[...] = flat[...].astype(bf16)
    else:
        for d in range(g_out.shape[0]):
            g_out[d] = flat[d * g_out.shape[1] : (d + 1) * g_out.shape[1], :].astype(bf16)


def potential_kernel(near, far, down, base, inside, out, order, field, total):
    leaf_dev = near.shape[1] // out.shape[0]
    lanes = OCT * 128
    copies = jnp.where(
        lax.broadcasted_iota(jnp.int32, (128, lanes), 1) // OCT
        == lax.broadcasted_iota(jnp.int32, (128, lanes), 0),
        1.0,
        0.0,
    ).astype(bf16)
    for at in range(far.shape[1] // 128):
        parent = nn(far[:, at * 128 : (at + 1) * 128].astype(bf16), copies).astype(bf16)
        child = nn(down[...], by_octant(parent))
        columns = slice(at * lanes, (at + 1) * lanes)
        expansion = (near[:, columns] + child).astype(bf16)
        for c in range(OCT):
            field[c * KP : (c + 1) * KP, :] = expansion[:, c * leaf_dev : (c + 1) * leaf_dev]
        for c in range(OCT):
            row = at * OCT + c
            per_atom = nn(field[c * KP : (c + 1) * KP, :], inside[...])
            total[row : row + 1, :] = jnp.sum(base[...] * per_atom, axis=0, keepdims=True)
    out[...] = total[...].astype(bf16)
    order[...] = turned_order()


def turned_order():
    size = FOUR * 128
    row = lax.broadcasted_iota(jnp.int32, (size, size), 0)
    k, level, group, at = row // 16 % FOUR, row // GROUP % 2, row % GROUP, row // 64
    wanted = k * 128 + level * 64 + slot_of(group, at)
    return jnp.where(lax.broadcasted_iota(jnp.int32, (size, size), 1) == wanted, 1.0, 0.0).astype(bf16)


def reduce_kernel(parts, after, order, out, total, laid):
    summed = parts[0].astype(f32)
    for d in range(1, parts.shape[0]):
        summed = summed + parts[d].astype(f32)
    total[...] = summed
    count = summed.shape[0] // FOUR
    tiles = [total[pl.ds(tile, count, stride=FOUR), :] for tile in range(FOUR)]
    turned = nn(jnp.concatenate(tiles, axis=1).astype(bf16), order[...])
    for k in range(FOUR):
        laid[pl.ds(k, count, stride=FOUR), :] = turned[:, k * 128 : (k + 1) * 128]
    for d in range(out.shape[0]):
        out[d] = laid[...].astype(bf16)


def unpack_kernel(whole, leaf_out, coarse_out, flat):
    kcount, jcount, slots = leaf_out.shape
    if len(whole.shape) == 2:
        flat[...] = whole[...].astype(f32)
    else:
        for d in range(whole.shape[0]):
            flat[d * whole.shape[1] : (d + 1) * whole.shape[1], :] = whole[d].astype(f32)
    for k in range(kcount):
        row = flat[pl.ds(k // FOUR * FOUR * jcount + k % FOUR, jcount, stride=FOUR), :]
        leaf_out[k] = row[:, 0:slots]
        coarse_out[k] = pltpu.roll(row, slots, 1)[:, 0:slots]


def mixing_kernel(whole, mix, charges, out, mixed):
    part = out.shape[0]
    me = lax.axis_index("chan")
    mixed[...] = lax.dot_general(
        mix[...], whole[...], (((0,), (0,)), ((), ())), preferred_element_type=f32
    )
    out[...] = (charges[...].astype(f32) + mixed[pl.ds(me * part, part), :]).astype(bf16)


def call(kernel, outs, scratch, flops=10**8, moved=10**6, limit=VMEM_BYTES, **kw):
    return pl.pallas_call(
        kernel,
        out_shape=outs,
        scratch_shapes=scratch,
        compiler_params=pltpu.CompilerParams(vmem_limit_bytes=limit),
        cost_estimate=pl.CostEstimate(flops=flops, bytes_accessed=moved, transcendentals=0),
        **kw,
    )


def from_chan(block):
    count = lax.axis_size("chan")
    return [lax.ppermute(block, "chan", [(i, i ^ d) for i in range(count)]) for d in range(1, count)]


def local(
    charges, basis, atom_leaf, leaf_lists, coarse_lists, up_ops, down_ops, leaf_ops, coarse_ops, mix, cotangent
):
    part, atoms = charges.shape
    kcount = basis.shape[0]
    slots, leaf_dev = leaf_lists.shape
    rows = part * kcount
    coarse_rows = rows // OCT
    steps = slots // GROUP
    cells = lax.axis_size("cells")
    devices = cells * lax.axis_size("chan")
    leaf = atom_leaf.reshape(1, atoms)
    shape = jax.ShapeDtypeStruct
    far_off = pl.BlockSpec(memory_space=pltpu.HBM)
    near_by = pl.BlockSpec(memory_space=pltpu.VMEM)
    like = lambda a: pltpu.VMEM(a.shape, a.dtype)
    stay = lambda *arrays: [pltpu.with_memory_space_constraint(a, pltpu.HBM) for a in arrays]
    wide = part * leaf_dev

    cot = from_chan(cotangent)
    held = (
        cotangent,
        mix,
        jnp.swapaxes(up_ops, 0, 1),
        jnp.swapaxes(down_ops, 0, 1),
        leaf_ops,
        coarse_ops,
        leaf_lists,
        coarse_lists.T,
    )
    m, first, second, base, inside, charges_near, *held = call(
        moments_kernel,
        (
            shape((rows, leaf_dev), bf16),
            shape((rows // 2, leaf_dev), bf16),
            shape((rows // 2, leaf_dev), bf16),
            shape((KP, atoms), f32),
            shape((leaf_dev, atoms), bf16),
            shape(charges.shape, bf16),
            *[shape(a.shape, a.dtype) for a in held],
        ),
        [like(basis), like(leaf), pltpu.VMEM((rows, atoms), bf16), pltpu.SemaphoreType.DMA((3 + MORE,))],
        in_specs=[far_off] * (3 + MORE),
    )(*stay(charges, basis, leaf, *held))
    inner = [(i, i + 1) for i in range(1, cells - 1, 2)]
    outer = [(i, i + 1) for i in range(0, cells - 1, 2)]
    first = lax.ppermute(first, "cells", inner + [(b, a) for a, b in inner])
    second = lax.ppermute(second, "cells", outer + [(b, a) for a, b in outer])
    own, mix_near, *prepared = held

    wide_ops = shape((KP, OCT * KP), bf16)
    group_ops = shape((steps, KP, GROUP * KP), bf16)
    cc, up, down, back_ops, lops, cops, idx, idxc = call(
        prepare_kernel,
        (
            shape((coarse_rows, 128), bf16),
            wide_ops,
            wide_ops,
            wide_ops,
            group_ops,
            group_ops,
            shape((slots, 128), jnp.int32),
            shape((slots, 128), jnp.int32),
        ),
        [
            pltpu.VMEM((KP, wide), bf16),
            pltpu.VMEM((2, OCT, KP, 128), f32),
            pltpu.VMEM((kcount, KP, 128), f32),
            pltpu.VMEM((KP, slots, KP), f32),
            pltpu.VMEM((128, OCT * 128), bf16),
        ],
    )(*prepared, m)
    be, bf = call(
        back_kernel,
        (shape((KP, wide), bf16), shape((KP, wide // OCT), bf16)),
        [
            pltpu.VMEM((rows, atoms), bf16),
            pltpu.VMEM((mix.shape[0], atoms), bf16),
            pltpu.VMEM((128, OCT * 128), bf16),
        ],
    )(own, *cot, mix_near, base, inside, back_ops)

    flat_rows = -(-(-(-kcount // FOUR) * FOUR * kcount) // 256) * 256
    fits = flat_rows % (8 * devices) == 0
    laid = (devices, flat_rows // devices, 128) if fits else (flat_rows, 128)
    near, far, grads = call(
        functools.partial(grads_kernel, kcount=kcount),
        (shape((KP, wide), f32), shape((KP, wide // OCT), f32), shape(laid, bf16)),
        [
            pltpu.VMEM((rows, 2 * leaf_dev), bf16),
            pltpu.VMEM((coarse_rows, 256), bf16),
            pltpu.VMEM((KP, wide), bf16),
            pltpu.VMEM((GROUP * KM + 16, wide), bf16),
            pltpu.VMEM((GROUP * KM + 16, wide), bf16),
            pltpu.VMEM((GROUP * KM + 16, wide // OCT), bf16),
            pltpu.VMEM((GROUP * KM + 16, wide // OCT), bf16),
            pltpu.VMEM((16, wide), f32),
            pltpu.VMEM((16, wide), f32),
            pltpu.VMEM((16, wide // OCT), f32),
            pltpu.VMEM((16, wide // OCT), f32),
            pltpu.VMEM((128, OCT * 128), bf16),
            pltpu.VMEM((2 * steps, KP, GROUP * KP), f32),
            pltpu.VMEM((flat_rows, 128), f32),
        ],
    )(m, first, second, cc, be, bf, up, idx, idxc, lops, cops)
    potential, order = call(
        potential_kernel,
        (shape((part, atoms), bf16), shape((FOUR * 128, FOUR * 128), bf16)),
        [pltpu.VMEM((OCT * KP, leaf_dev), bf16), pltpu.VMEM((part, atoms), f32)],
    )(near, far, down, base, inside)

    axes = ("cells", "chan")
    if fits:
        parts = lax.all_to_all(grads, axes, 0, 0)
        spread_out = call(
            reduce_kernel,
            shape(laid, bf16),
            [pltpu.VMEM(laid[1:], f32), pltpu.VMEM(laid[1:], f32)],
            in_specs=[near_by, pl.BlockSpec(memory_space=pl.ANY), near_by],
        )(parts, potential, order)
        whole = lax.all_to_all(spread_out, axes, 0, 0)
    else:
        split = -(-flat_rows // devices) * devices
        pieces = jnp.pad(grads, ((0, split - flat_rows), (0, 0))).reshape(devices, -1, 128)
        parts = lax.all_to_all(pieces, axes, 0, 0)
        mine = jnp.sum(parts.astype(f32), axis=0).astype(bf16)
        whole = lax.all_gather(mine, axes).reshape(split, 128)[:flat_rows]
        whole = whole.reshape(flat_rows // FOUR, FOUR, 2, FOUR, 2, GROUP)
        whole = jnp.transpose(whole, (0, 3, 4, 1, 2, 5)).reshape(flat_rows, 128)
    grad_shape = shape((kcount, kcount, slots), f32)
    grad_leaf, grad_coarse = call(
        unpack_kernel, (grad_shape, grad_shape), [pltpu.VMEM((flat_rows, 128), f32)]
    )(whole)

    refined = call(
        mixing_kernel,
        shape((part, atoms), bf16),
        [pltpu.VMEM((mix.shape[0], atoms), f32)],
    )(lax.all_gather(potential, "chan", axis=0, tiled=True), mix_near, charges_near)
    return refined, grad_leaf, grad_coarse


def solution(mesh):
    placed = (
        P("chan", "cells"),
        P(None, "cells"),
        P("cells"),
        P(None, "cells"),
        P(None, "cells"),
        P(),
        P(),
        P(),
        P(),
        P(),
        P("chan", "cells"),
    )
    return jax.shard_map(
        local, mesh=mesh, in_specs=placed, out_specs=(P("chan", "cells"), P(), P()), check_vma=False
    )
```

```python
import functools

import jax
import jax.numpy as jnp
from jax import lax
from jax.experimental import pallas as pl
from jax.experimental.pallas import tpu as pltpu
from jax.sharding import PartitionSpec as P

KP = 32
GROUP = 8
KM = 24
CHUNK = 8
FOUR = 4
OCT = 8
MORE = 8
VMEM_BYTES = 24 * 1024 * 1024
f32 = jnp.float32
bf16 = jnp.bfloat16


def nt(a, b):
    return lax.dot_general(a, b, (((1,), (1,)), ((), ())), preferred_element_type=f32)


def nn(a, b):
    return jnp.dot(a, b, preferred_element_type=f32)


def member(leaf_row, leaf_dev):
    shape = (leaf_dev, leaf_row.shape[1])
    return jnp.where(lax.broadcasted_iota(jnp.int32, shape, 0) == leaf_row, 1.0, 0.0).astype(bf16)


def spread(base, values, scaled):
    wide = values.astype(f32)
    count = values.shape[0]
    for c in range(0, count, 2):
        pair = [base[0:KM, :] * wide[c + i : c + i + 1, :] for i in range(2)]
        scaled[c * KM : (c + 2) * KM, :] = jnp.concatenate(pair, axis=0).astype(bf16)
    scaled[count * KM :, :] = (base[KM : KM + 1, :] * wide).astype(bf16)


def lay_wide(rows, out):
    count = rows.shape[0] // (KM + 1)
    lanes = rows.shape[1]
    top = lax.broadcasted_iota(jnp.int32, (KP - KM, lanes), 0) == 0
    for c in range(count):
        last = jnp.where(top, rows[count * KM + c : count * KM + c + 1, :], 0.0)
        block = jnp.concatenate([rows[c * KM : (c + 1) * KM, :], last], axis=0)
        out[:, c * lanes : (c + 1) * lanes] = block.astype(bf16)


def fetch(pairs, sems):
    copies = [pltpu.make_async_copy(src, dst, sems.at[i]) for i, (src, dst) in enumerate(pairs)]
    for copy in copies:
        copy.start()
    return copies


def pooling(rows, cols):
    return jnp.where(
        lax.broadcasted_iota(jnp.int32, (rows, cols), 0) // OCT
        == lax.broadcasted_iota(jnp.int32, (rows, cols), 1),
        1.0,
        0.0,
    ).astype(bf16)


def by_octant(values):
    octant = lax.broadcasted_iota(jnp.int32, (1, values.shape[1]), 1) % OCT
    return jnp.concatenate(
        [values * jnp.where(octant == o, 1.0, 0.0).astype(values.dtype) for o in range(OCT)], axis=0
    )


def upward(ops, wide_ref, sums, pool):
    lanes = OCT * 128
    for part in range(wide_ref.shape[1] // lanes):
        spaced = by_octant(wide_ref[:, part * lanes : (part + 1) * lanes])
        sums[part * KP : (part + 1) * KP, :] = nn(ops, spaced).astype(bf16)
    return nn(sums[...], pool[...])


def tightened(rows):
    count = rows.shape[0] // KP
    whole = [rows[c * KP : c * KP + KM] for c in range(count)]
    last = [rows[c * KP + KM : c * KP + KM + 1] for c in range(count)]
    return jnp.concatenate(whole + last, axis=0).astype(bf16)


def moments_kernel(charges_hbm, basis_hbm, leaf_hbm, *rest):
    more = rest[:MORE]
    m_out, first_out, second_out, base_out, inside_out, pool_out, charges = rest[MORE : MORE + 7]
    held = rest[MORE + 7 : 2 * MORE + 7]
    basis, leaf, scaled, sems = rest[2 * MORE + 7 :]
    leaf_dev = m_out.shape[1]
    half = leaf_dev // 2
    cell = lax.axis_index("cells")
    copies = fetch(
        [(charges_hbm, charges), (basis_hbm, basis), (leaf_hbm, leaf), *zip(more, held)], sems
    )
    kcount = basis.shape[0]
    base_out[...] = jnp.zeros_like(base_out)
    pool_out[...] = pooling(*pool_out.shape)
    for copy in copies[:3]:
        copy.wait()
    base_out[0:kcount, :] = basis[...]
    inside_out[...] = member(leaf[...] - cell * leaf_dev, leaf_dev)
    spread(base_out, charges[...], scaled)
    m = nt(scaled[...], inside_out[...])
    m_out[...] = m.astype(bf16)
    rows = m.shape[0] // 2
    upper, lower = m[:rows], m[rows:]
    low_lane = lax.broadcasted_iota(jnp.int32, (rows, leaf_dev), 1) < half
    hi = jnp.where(low_lane, pltpu.roll(upper, half, 1), lower).astype(bf16)
    lo = jnp.where(low_lane, upper, pltpu.roll(lower, half, 1)).astype(bf16)
    odd = lax.rem(cell, 2)
    first_out[...] = jnp.where(odd == 1, hi, lo)
    second_out[...] = jnp.where(odd == 1, lo, hi)
    for copy in copies[3:]:
        copy.wait()


def slot_of(group, at):
    return at * GROUP + group


def slot_ops(ops, padded, turned, out):
    kcount, jcount, slots = ops.shape
    turned[...] = jnp.zeros_like(turned)
    padded[...] = jnp.zeros_like(padded)
    for k in range(kcount):
        padded[k, 0:jcount, 0:slots] = ops[k].astype(f32)
        turned[k, :, :] = padded[k].T[0:slots]
    for group in range(out.shape[0]):
        held = [turned[:, slot_of(group, at), :] for at in range(GROUP)]
        pieces = [a[:, 0:KM] for a in held] + [a[:, KM : KM + 1] for a in held]
        pieces.append(jnp.zeros((KP, GROUP * KP - GROUP * (KM + 1)), f32))
        out[group] = jnp.concatenate(pieces, axis=1).astype(bf16)


def prepare_kernel(
    up,
    down,
    lops,
    cops,
    ll,
    cl,
    m,
    pool,
    cc_out,
    up_out,
    down_out,
    back_out,
    lops_out,
    cops_out,
    idx,
    idxc,
    wide,
    stack,
    padded,
    turned,
    sums,
):
    leaf_dev = m.shape[1]
    half = leaf_dev // 2
    kcount = up.shape[0]
    coarse_dev, slots = cl.shape
    cell = lax.axis_index("cells")
    lay_wide(m[...].astype(f32), wide)
    stack[...] = jnp.zeros_like(stack)
    for k in range(kcount):
        stack[0, :, k, 0:kcount] = up[k].astype(f32)
        stack[1, :, k, 0:kcount] = down[k].astype(f32)

    def side_by_side(pieces):
        return jnp.concatenate(pieces, axis=1).astype(bf16)

    up_out[...] = side_by_side([stack[0, o, :, 0:KP] for o in range(OCT)])
    down_out[...] = side_by_side([stack[1, o, :, 0:KP] for o in range(OCT)])
    back_out[...] = side_by_side([stack[1, o].T[0:KP, :] for o in range(OCT)])
    cc_out[...] = tightened(upward(up_out[...], wide, sums, pool))

    slot_ops(lops, padded, turned, lops_out)
    slot_ops(cops, padded, turned, cops_out)
    rel = ll[...] - cell * leaf_dev
    place = jnp.where(rel < 0, rel + leaf_dev + half, jnp.where(rel < leaf_dev, rel, rel + half))
    idx[...] = jnp.where(ll[...] < 0, -1, place)
    crel = cl[...] - cell * coarse_dev
    side = coarse_dev // 2
    cplace = jnp.where(crel < 0, crel + 128 + side, jnp.where(crel < coarse_dev, crel, crel + 128 - side))
    cplace = jnp.where(cl[...] < 0, -1, cplace).astype(f32).astype(bf16)
    copied = jnp.where(
        lax.broadcasted_iota(jnp.int32, (coarse_dev, 128), 0)
        == lax.broadcasted_iota(jnp.int32, (coarse_dev, 128), 1) % coarse_dev,
        1.0,
        0.0,
    ).astype(bf16)
    spot = lax.dot_general(cplace, copied, (((0,), (0,)), ((), ())), preferred_element_type=f32)
    spot = spot.astype(jnp.int32)
    start = lax.broadcasted_iota(jnp.int32, (slots, 128), 1) // coarse_dev * coarse_dev
    idxc[...] = jnp.where(spot < 0, -1, spot + start)


def back_kernel(own, core, cross, other, mix, base, inside, pool, back_ops, be_out, bf_out, scaled, gathered, sums):
    part = own.shape[0]
    me = lax.axis_index("chan")
    gathered[pl.ds(me * part, part), :] = own[...]
    gathered[pl.ds((me ^ 1) * part, part), :] = core[...]
    gathered[pl.ds((me ^ 2) * part, part), :] = cross[...]
    gathered[pl.ds((me ^ 3) * part, part), :] = other[...]
    potential = nn(mix[pl.ds(me * part, part), :], gathered[...]).astype(bf16)
    spread(base, potential, scaled)
    lay_wide(nt(scaled[...], inside[...]), be_out)
    far = upward(back_ops[...], be_out, sums, pool).astype(bf16)
    for at in range(far.shape[0] // KP):
        bf_out[:, at * 128 : (at + 1) * 128] = far[at * KP : (at + 1) * KP, :]


def grads_kernel(
    m,
    first,
    second,
    cc,
    be,
    bf,
    up,
    idx,
    idxc,
    lops,
    cops,
    pool,
    near,
    far,
    g_out,
    src,
    srcc,
    wide,
    even,
    odd,
    even_c,
    odd_c,
    even_last,
    odd_last,
    even_c_last,
    odd_c_last,
    sums,
    blocks,
    flat,
    *,
    kcount,
):
    leaf_dev = m.shape[1]
    half = leaf_dev // 2
    window = 2 * leaf_dev
    channels = m.shape[0] // kcount
    steps = idx.shape[0] // GROUP
    tight = even.shape[0]
    is_odd = lax.rem(lax.axis_index("cells"), 2) == 1

    src[:, 0:leaf_dev] = m[...]
    mid = first.shape[0]
    a, b = first[...].astype(f32), second[...].astype(f32)
    low, high = jnp.where(is_odd, b, a), jnp.where(is_odd, a, b)
    low_lane = lax.broadcasted_iota(jnp.int32, (mid, leaf_dev), 1) < half
    upper = jnp.where(low_lane, low, pltpu.roll(high, half, 1))
    lower = jnp.where(low_lane, pltpu.roll(low, half, 1), high)
    src[0:mid, leaf_dev:] = upper.astype(bf16)
    src[mid:, leaf_dev:] = lower.astype(bf16)
    lay_wide(src[:, leaf_dev:].astype(f32), wide)
    srcc[:, 0:128] = cc[...]
    srcc[:, 128:] = tightened(upward(up[...], wide, sums, pool))
    place_of = lax.broadcasted_iota(jnp.int32, (window, 128), 0)

    def chosen(ref, group, at):
        row = ref[pl.ds(slot_of(group, at), 1), :]
        return jnp.where(place_of == row, 1.0, 0.0).astype(bf16)

    def picks(source, ref, group, held, last, chunk):
        count = source.shape[0] // kcount
        for pair in range(GROUP // 2):
            at = 2 * pair
            both = jnp.concatenate([chosen(ref, group, at), chosen(ref, group, at + 1)], axis=1)
            for begin in range(0, count, chunk):
                end = begin + chunk
                end_row = end * KM if end < count else source.shape[0]
                picked = nn(source[begin * KM : end_row, :], both)
                for c in range(chunk):
                    rows = picked[c * KM : (c + 1) * KM]
                    lane = (begin + c) * 128
                    held[at * KM : (at + 2) * KM, lane : lane + 128] = jnp.concatenate(
                        [rows[:, 0:128], rows[:, 128:]], axis=0
                    ).astype(bf16)
            rows = picked[chunk * KM :]
            for i in range(2):
                for c in range(count):
                    last[at + i : at + i + 1, c * 128 : (c + 1) * 128] = rows[c : c + 1, i * 128 : (i + 1) * 128]
        held[GROUP * KM :, :] = last[...].astype(bf16)

    def pick_group(group, held, last, held_c, last_c):
        picks(src, idx, group, held, last, CHUNK)
        picks(srcc, idxc, group, held_c, last_c, srcc.shape[0] // kcount)

    def products(group, held, held_c):
        blocks[group, :, 0:tight] = nt(be[...], held[...])
        blocks[steps + group, :, 0:tight] = nt(bf[...], held_c[...])
        near[...] += nn(lops[group][:, 0:tight], held[...])
        far[...] += nn(cops[group][:, 0:tight], held_c[...])

    for ref in (near, far, even_last, odd_last, even_c_last, odd_c_last):
        ref[...] = jnp.zeros_like(ref)
    evens, odds = (even, even_last, even_c, even_c_last), (odd, odd_last, odd_c, odd_c_last)
    pick_group(0, *evens)

    def two_groups(i, carry):
        group = 2 * i + 1
        pick_group(group, *odds)
        products(group - 1, even, even_c)
        pick_group(group + 1, *evens)
        products(group, odd, odd_c)
        return carry

    lax.fori_loop(0, steps // 2 - 1, two_groups, 0)
    pick_group(steps - 1, *odds)
    products(steps - 2, even, even_c)
    products(steps - 1, odd, odd_c)
    flat[...] = jnp.zeros_like(flat)
    main = GROUP * KM
    for turn in range(-(-kcount // FOUR)):
        several = jnp.concatenate([blocks[:, turn * FOUR + k, :] for k in range(FOUR)], axis=0)
        across = several.T
        for tile in range(GROUP // 2):
            at = 2 * tile
            body = jnp.concatenate([across[a * KM : (a + 1) * KM] for a in (at, at + 1)], axis=1)
            rest = jnp.concatenate([across[main + a : main + a + 1] for a in (at, at + 1)], axis=1)
            rows = pl.ds(turn * FOUR * kcount + tile, kcount, stride=FOUR)
            flat[rows, :] = jnp.concatenate([body, rest], axis=0)
    if len(g_out.shape) == 2:
        g_out[...] = flat[...].astype(bf16)
    else:
        for d in range(g_out.shape[0]):
            g_out[d] = flat[d * g_out.shape[1] : (d + 1) * g_out.shape[1], :].astype(bf16)


def potential_kernel(near, far, down, base, inside, out, order, field, total):
    leaf_dev = near.shape[1] // out.shape[0]
    lanes = OCT * 128
    copies = jnp.where(
        lax.broadcasted_iota(jnp.int32, (128, lanes), 1) // OCT
        == lax.broadcasted_iota(jnp.int32, (128, lanes), 0),
        1.0,
        0.0,
    ).astype(bf16)
    for at in range(far.shape[1] // 128):
        parent = nn(far[:, at * 128 : (at + 1) * 128].astype(bf16), copies).astype(bf16)
        child = nn(down[...], by_octant(parent))
        columns = slice(at * lanes, (at + 1) * lanes)
        expansion = (near[:, columns] + child).astype(bf16)
        for c in range(OCT):
            field[c * KP : (c + 1) * KP, :] = expansion[:, c * leaf_dev : (c + 1) * leaf_dev]
        for c in range(OCT):
            row = at * OCT + c
            per_atom = nn(field[c * KP : (c + 1) * KP, :], inside[...])
            total[row : row + 1, :] = jnp.sum(base[...] * per_atom, axis=0, keepdims=True)
    out[...] = total[...].astype(bf16)
    order[...] = turned_order()


def turned_order():
    size = FOUR * 128
    row = lax.broadcasted_iota(jnp.int32, (size, size), 0)
    k, level, group, at = row // 16 % FOUR, row // GROUP % 2, row % GROUP, row // 64
    wanted = k * 128 + level * 64 + slot_of(group, at)
    return jnp.where(lax.broadcasted_iota(jnp.int32, (size, size), 1) == wanted, 1.0, 0.0).astype(bf16)


def reduce_kernel(parts, after, order, out, total, laid):
    summed = parts[0].astype(f32)
    for d in range(1, parts.shape[0]):
        summed = summed + parts[d].astype(f32)
    total[...] = summed
    count = summed.shape[0] // FOUR
    tiles = [total[pl.ds(tile, count, stride=FOUR), :] for tile in range(FOUR)]
    turned = nn(jnp.concatenate(tiles, axis=1).astype(bf16), order[...])
    for k in range(FOUR):
        laid[pl.ds(k, count, stride=FOUR), :] = turned[:, k * 128 : (k + 1) * 128]
    for d in range(out.shape[0]):
        out[d] = laid[...].astype(bf16)


def unpack_kernel(whole, leaf_out, coarse_out, flat):
    kcount, jcount, slots = leaf_out.shape
    if len(whole.shape) == 2:
        flat[...] = whole[...].astype(f32)
    else:
        for d in range(whole.shape[0]):
            flat[d * whole.shape[1] : (d + 1) * whole.shape[1], :] = whole[d].astype(f32)
    for k in range(kcount):
        row = flat[pl.ds(k // FOUR * FOUR * jcount + k % FOUR, jcount, stride=FOUR), :]
        leaf_out[k] = row[:, 0:slots]
        coarse_out[k] = pltpu.roll(row, slots, 1)[:, 0:slots]


def mixing_kernel(whole, mix, charges, out, mixed):
    part = out.shape[0]
    me = lax.axis_index("chan")
    mixed[...] = lax.dot_general(
        mix[...], whole[...], (((0,), (0,)), ((), ())), preferred_element_type=f32
    )
    out[...] = (charges[...].astype(f32) + mixed[pl.ds(me * part, part), :]).astype(bf16)


def call(kernel, outs, scratch, flops=10**8, moved=10**6, limit=VMEM_BYTES, **kw):
    return pl.pallas_call(
        kernel,
        out_shape=outs,
        scratch_shapes=scratch,
        compiler_params=pltpu.CompilerParams(vmem_limit_bytes=limit),
        cost_estimate=pl.CostEstimate(flops=flops, bytes_accessed=moved, transcendentals=0),
        **kw,
    )


def from_chan(block):
    count = lax.axis_size("chan")

    def swap(part, d):
        return lax.ppermute(part, "chan", [(i, i ^ d) for i in range(count)])

    cross = swap(block, 2)
    return [swap(block, 1), cross, swap(cross, 1)]


def local(
    charges, basis, atom_leaf, leaf_lists, coarse_lists, up_ops, down_ops, leaf_ops, coarse_ops, mix, cotangent
):
    part, atoms = charges.shape
    kcount = basis.shape[0]
    slots, leaf_dev = leaf_lists.shape
    rows = part * kcount
    coarse_rows = rows // OCT
    steps = slots // GROUP
    cells = lax.axis_size("cells")
    devices = cells * lax.axis_size("chan")
    leaf = atom_leaf.reshape(1, atoms)
    shape = jax.ShapeDtypeStruct
    far_off = pl.BlockSpec(memory_space=pltpu.HBM)
    near_by = pl.BlockSpec(memory_space=pltpu.VMEM)
    like = lambda a: pltpu.VMEM(a.shape, a.dtype)
    stay = lambda *arrays: [pltpu.with_memory_space_constraint(a, pltpu.HBM) for a in arrays]
    wide = part * leaf_dev

    cot = from_chan(cotangent)
    held = (
        cotangent,
        mix,
        jnp.swapaxes(up_ops, 0, 1),
        jnp.swapaxes(down_ops, 0, 1),
        leaf_ops,
        coarse_ops,
        leaf_lists,
        coarse_lists.T,
    )
    m, first, second, base, inside, pool, charges_near, *held = call(
        moments_kernel,
        (
            shape((rows, leaf_dev), bf16),
            shape((rows // 2, leaf_dev), bf16),
            shape((rows // 2, leaf_dev), bf16),
            shape((KP, atoms), f32),
            shape((leaf_dev, atoms), bf16),
            shape((OCT * 128, 128), bf16),
            shape(charges.shape, bf16),
            *[shape(a.shape, a.dtype) for a in held],
        ),
        [like(basis), like(leaf), pltpu.VMEM((rows, atoms), bf16), pltpu.SemaphoreType.DMA((3 + MORE,))],
        in_specs=[far_off] * (3 + MORE),
    )(*stay(charges, basis, leaf, *held))
    inner = [(i, i + 1) for i in range(1, cells - 1, 2)]
    outer = [(i, i + 1) for i in range(0, cells - 1, 2)]
    first = lax.ppermute(first, "cells", inner + [(b, a) for a, b in inner])
    second = lax.ppermute(second, "cells", outer + [(b, a) for a, b in outer])
    own, mix_near, *prepared = held

    wide_ops = shape((KP, OCT * KP), bf16)
    group_ops = shape((steps, KP, GROUP * KP), bf16)
    cc, up, down, back_ops, lops, cops, idx, idxc = call(
        prepare_kernel,
        (
            shape((coarse_rows, 128), bf16),
            wide_ops,
            wide_ops,
            wide_ops,
            group_ops,
            group_ops,
            shape((slots, 128), jnp.int32),
            shape((slots, 128), jnp.int32),
        ),
        [
            pltpu.VMEM((KP, wide), bf16),
            pltpu.VMEM((2, OCT, KP, 128), f32),
            pltpu.VMEM((kcount, KP, 128), f32),
            pltpu.VMEM((KP, slots, KP), f32),
            pltpu.VMEM((128, OCT * 128), bf16),
        ],
        flops=2 * 10**9,
    )(*prepared, m, pool)
    be, bf = call(
        back_kernel,
        (shape((KP, wide), bf16), shape((KP, wide // OCT), bf16)),
        [
            pltpu.VMEM((rows, atoms), bf16),
            pltpu.VMEM((mix.shape[0], atoms), bf16),
            pltpu.VMEM((128, OCT * 128), bf16),
        ],
    )(own, *cot, mix_near, base, inside, pool, back_ops)

    flat_rows = -(-(-(-kcount // FOUR) * FOUR * kcount) // 256) * 256
    fits = flat_rows % (8 * devices) == 0
    laid = (devices, flat_rows // devices, 128) if fits else (flat_rows, 128)
    near, far, grads = call(
        functools.partial(grads_kernel, kcount=kcount),
        (shape((KP, wide), f32), shape((KP, wide // OCT), f32), shape(laid, bf16)),
        [
            pltpu.VMEM((rows, 2 * leaf_dev), bf16),
            pltpu.VMEM((coarse_rows, 256), bf16),
            pltpu.VMEM((KP, wide), bf16),
            pltpu.VMEM((GROUP * KM + 16, wide), bf16),
            pltpu.VMEM((GROUP * KM + 16, wide), bf16),
            pltpu.VMEM((GROUP * KM + 16, wide // OCT), bf16),
            pltpu.VMEM((GROUP * KM + 16, wide // OCT), bf16),
            pltpu.VMEM((16, wide), f32),
            pltpu.VMEM((16, wide), f32),
            pltpu.VMEM((16, wide // OCT), f32),
            pltpu.VMEM((16, wide // OCT), f32),
            pltpu.VMEM((128, OCT * 128), bf16),
            pltpu.VMEM((2 * steps, KP, GROUP * KP), f32),
            pltpu.VMEM((flat_rows, 128), f32),
        ],
    )(m, first, second, cc, be, bf, up, idx, idxc, lops, cops, pool)
    potential, order = call(
        potential_kernel,
        (shape((part, atoms), bf16), shape((FOUR * 128, FOUR * 128), bf16)),
        [pltpu.VMEM((OCT * KP, leaf_dev), bf16), pltpu.VMEM((part, atoms), f32)],
    )(near, far, down, base, inside)

    axes = ("cells", "chan")
    if fits:
        parts = lax.all_to_all(grads, axes, 0, 0)
        spread_out = call(
            reduce_kernel,
            shape(laid, bf16),
            [pltpu.VMEM(laid[1:], f32), pltpu.VMEM(laid[1:], f32)],
            in_specs=[near_by, pl.BlockSpec(memory_space=pl.ANY), near_by],
        )(parts, potential, order)
        whole = lax.all_to_all(spread_out, axes, 0, 0)
    else:
        split = -(-flat_rows // devices) * devices
        pieces = jnp.pad(grads, ((0, split - flat_rows), (0, 0))).reshape(devices, -1, 128)
        parts = lax.all_to_all(pieces, axes, 0, 0)
        mine = jnp.sum(parts.astype(f32), axis=0).astype(bf16)
        whole = lax.all_gather(mine, axes).reshape(split, 128)[:flat_rows]
        whole = whole.reshape(flat_rows // FOUR, FOUR, 2, FOUR, 2, GROUP)
        whole = jnp.transpose(whole, (0, 3, 4, 1, 2, 5)).reshape(flat_rows, 128)
    grad_shape = shape((kcount, kcount, slots), f32)
    grad_leaf, grad_coarse = call(
        unpack_kernel, (grad_shape, grad_shape), [pltpu.VMEM((flat_rows, 128), f32)]
    )(whole)

    refined = call(
        mixing_kernel,
        shape((part, atoms), bf16),
        [pltpu.VMEM((mix.shape[0], atoms), f32)],
    )(lax.all_gather(potential, "chan", axis=0, tiled=True), mix_near, charges_near)
    return refined, grad_leaf, grad_coarse


def solution(mesh):
    placed = (
        P("chan", "cells"),
        P(None, "cells"),
        P("cells"),
        P(None, "cells"),
        P(None, "cells"),
        P(),
        P(),
        P(),
        P(),
        P(),
        P("chan", "cells"),
    )
    return jax.shard_map(
        local, mesh=mesh, in_specs=placed, out_specs=(P("chan", "cells"), P(), P()), check_vma=False
    )
```

```python
import functools

import jax
import jax.numpy as jnp
from jax import lax
from jax.experimental import pallas as pl
from jax.experimental.pallas import tpu as pltpu
from jax.sharding import PartitionSpec as P

KP = 32
GROUP = 8
KM = 24
CHUNK = 16
FOUR = 4
OCT = 8
MORE = 8
VMEM_BYTES = 24 * 1024 * 1024
f32 = jnp.float32
bf16 = jnp.bfloat16


def nt(a, b):
    return lax.dot_general(a, b, (((1,), (1,)), ((), ())), preferred_element_type=f32)


def nn(a, b):
    return jnp.dot(a, b, preferred_element_type=f32)


def member(leaf_row, leaf_dev):
    shape = (leaf_dev, leaf_row.shape[1])
    return jnp.where(lax.broadcasted_iota(jnp.int32, shape, 0) == leaf_row, 1.0, 0.0).astype(bf16)


def spread(base, values, scaled):
    wide = values.astype(f32)
    count = values.shape[0]
    for c in range(0, count, 2):
        pair = [base[0:KM, :] * wide[c + i : c + i + 1, :] for i in range(2)]
        scaled[c * KM : (c + 2) * KM, :] = jnp.concatenate(pair, axis=0).astype(bf16)
    scaled[count * KM :, :] = (base[KM : KM + 1, :] * wide).astype(bf16)


def lay_wide(rows, out):
    count = rows.shape[0] // (KM + 1)
    lanes = rows.shape[1]
    top = lax.broadcasted_iota(jnp.int32, (KP - KM, lanes), 0) == 0
    for c in range(count):
        last = jnp.where(top, rows[count * KM + c : count * KM + c + 1, :], 0.0)
        block = jnp.concatenate([rows[c * KM : (c + 1) * KM, :], last], axis=0)
        out[:, c * lanes : (c + 1) * lanes] = block.astype(bf16)


def fetch(pairs, sems):
    copies = [pltpu.make_async_copy(src, dst, sems.at[i]) for i, (src, dst) in enumerate(pairs)]
    for copy in copies:
        copy.start()
    return copies


def pooling(rows, cols):
    return jnp.where(
        lax.broadcasted_iota(jnp.int32, (rows, cols), 0) // OCT
        == lax.broadcasted_iota(jnp.int32, (rows, cols), 1),
        1.0,
        0.0,
    ).astype(bf16)


def by_octant(values):
    octant = lax.broadcasted_iota(jnp.int32, (1, values.shape[1]), 1) % OCT
    return jnp.concatenate(
        [values * jnp.where(octant == o, 1.0, 0.0).astype(values.dtype) for o in range(OCT)], axis=0
    )


def upward(ops, wide_ref, sums, pool):
    lanes = OCT * 128
    for part in range(wide_ref.shape[1] // lanes):
        spaced = by_octant(wide_ref[:, part * lanes : (part + 1) * lanes])
        sums[part * KP : (part + 1) * KP, :] = nn(ops, spaced).astype(bf16)
    return nn(sums[...], pool[...])


def tightened(rows):
    count = rows.shape[0] // KP
    whole = [rows[c * KP : c * KP + KM] for c in range(count)]
    last = [rows[c * KP + KM : c * KP + KM + 1] for c in range(count)]
    return jnp.concatenate(whole + last, axis=0).astype(bf16)


def moments_kernel(charges_hbm, basis_hbm, leaf_hbm, *rest):
    more = rest[:MORE]
    m_out, first_out, second_out, base_out, inside_out, pool_out, charges = rest[MORE : MORE + 7]
    held = rest[MORE + 7 : 2 * MORE + 7]
    basis, leaf, scaled, sems = rest[2 * MORE + 7 :]
    leaf_dev = m_out.shape[1]
    half = leaf_dev // 2
    cell = lax.axis_index("cells")
    copies = fetch(
        [(charges_hbm, charges), (basis_hbm, basis), (leaf_hbm, leaf), *zip(more, held)], sems
    )
    kcount = basis.shape[0]
    base_out[...] = jnp.zeros_like(base_out)
    pool_out[...] = pooling(*pool_out.shape)
    for copy in copies[:3]:
        copy.wait()
    base_out[0:kcount, :] = basis[...]
    inside_out[...] = member(leaf[...] - cell * leaf_dev, leaf_dev)
    spread(base_out, charges[...], scaled)
    m = nt(scaled[...], inside_out[...])
    m_out[...] = m.astype(bf16)
    rows = m.shape[0] // 2
    upper, lower = m[:rows], m[rows:]
    low_lane = lax.broadcasted_iota(jnp.int32, (rows, leaf_dev), 1) < half
    hi = jnp.where(low_lane, pltpu.roll(upper, half, 1), lower).astype(bf16)
    lo = jnp.where(low_lane, upper, pltpu.roll(lower, half, 1)).astype(bf16)
    odd = lax.rem(cell, 2)
    first_out[...] = jnp.where(odd == 1, hi, lo)
    second_out[...] = jnp.where(odd == 1, lo, hi)
    for copy in copies[3:]:
        copy.wait()


def slot_of(group, at):
    return at * GROUP + group


def slot_ops(ops, padded, turned, out):
    kcount, jcount, slots = ops.shape
    turned[...] = jnp.zeros_like(turned)
    padded[...] = jnp.zeros_like(padded)
    for k in range(kcount):
        padded[k, 0:jcount, 0:slots] = ops[k].astype(f32)
        turned[k, :, :] = padded[k].T[0:slots]
    for group in range(out.shape[0]):
        held = [turned[:, slot_of(group, at), :] for at in range(GROUP)]
        pieces = [a[:, 0:KM] for a in held] + [a[:, KM : KM + 1] for a in held]
        pieces.append(jnp.zeros((KP, GROUP * KP - GROUP * (KM + 1)), f32))
        out[group] = jnp.concatenate(pieces, axis=1).astype(bf16)


def prepare_kernel(
    up,
    down,
    lops,
    cops,
    ll,
    cl,
    m,
    pool,
    cc_out,
    up_out,
    down_out,
    back_out,
    lops_out,
    cops_out,
    idx,
    idxc,
    wide,
    stack,
    padded,
    turned,
    sums,
):
    leaf_dev = m.shape[1]
    half = leaf_dev // 2
    kcount = up.shape[0]
    coarse_dev, slots = cl.shape
    cell = lax.axis_index("cells")
    lay_wide(m[...].astype(f32), wide)
    stack[...] = jnp.zeros_like(stack)
    for k in range(kcount):
        stack[0, :, k, 0:kcount] = up[k].astype(f32)
        stack[1, :, k, 0:kcount] = down[k].astype(f32)

    def side_by_side(pieces):
        return jnp.concatenate(pieces, axis=1).astype(bf16)

    up_out[...] = side_by_side([stack[0, o, :, 0:KP] for o in range(OCT)])
    down_out[...] = side_by_side([stack[1, o, :, 0:KP] for o in range(OCT)])
    back_out[...] = side_by_side([stack[1, o].T[0:KP, :] for o in range(OCT)])
    cc_out[...] = tightened(upward(up_out[...], wide, sums, pool))

    slot_ops(lops, padded, turned, lops_out)
    slot_ops(cops, padded, turned, cops_out)
    rel = ll[...] - cell * leaf_dev
    place = jnp.where(rel < 0, rel + leaf_dev + half, jnp.where(rel < leaf_dev, rel, rel + half))
    idx[...] = jnp.where(ll[...] < 0, -1, place)
    crel = cl[...] - cell * coarse_dev
    side = coarse_dev // 2
    cplace = jnp.where(crel < 0, crel + 128 + side, jnp.where(crel < coarse_dev, crel, crel + 128 - side))
    cplace = jnp.where(cl[...] < 0, -1, cplace).astype(f32).astype(bf16)
    copied = jnp.where(
        lax.broadcasted_iota(jnp.int32, (coarse_dev, 128), 0)
        == lax.broadcasted_iota(jnp.int32, (coarse_dev, 128), 1) % coarse_dev,
        1.0,
        0.0,
    ).astype(bf16)
    spot = lax.dot_general(cplace, copied, (((0,), (0,)), ((), ())), preferred_element_type=f32)
    spot = spot.astype(jnp.int32)
    start = lax.broadcasted_iota(jnp.int32, (slots, 128), 1) // coarse_dev * coarse_dev
    idxc[...] = jnp.where(spot < 0, -1, spot + start)


def back_kernel(own, core, cross, other, mix, base, inside, pool, back_ops, be_out, bf_out, scaled, gathered, sums):
    part = own.shape[0]
    me = lax.axis_index("chan")
    gathered[pl.ds(me * part, part), :] = own[...]
    gathered[pl.ds((me ^ 1) * part, part), :] = core[...]
    gathered[pl.ds((me ^ 2) * part, part), :] = cross[...]
    gathered[pl.ds((me ^ 3) * part, part), :] = other[...]
    potential = nn(mix[pl.ds(me * part, part), :], gathered[...]).astype(bf16)
    spread(base, potential, scaled)
    lay_wide(nt(scaled[...], inside[...]), be_out)
    far = upward(back_ops[...], be_out, sums, pool).astype(bf16)
    for at in range(far.shape[0] // KP):
        bf_out[:, at * 128 : (at + 1) * 128] = far[at * KP : (at + 1) * KP, :]


def grads_kernel(
    m,
    first,
    second,
    cc,
    be,
    bf,
    up,
    idx,
    idxc,
    lops,
    cops,
    pool,
    near,
    far,
    g_out,
    src,
    srcc,
    wide,
    even,
    odd,
    even_c,
    odd_c,
    even_last,
    odd_last,
    even_c_last,
    odd_c_last,
    sums,
    blocks,
    flat,
    *,
    kcount,
):
    leaf_dev = m.shape[1]
    half = leaf_dev // 2
    window = 2 * leaf_dev
    channels = m.shape[0] // kcount
    steps = idx.shape[0] // GROUP
    tight = even.shape[0]
    is_odd = lax.rem(lax.axis_index("cells"), 2) == 1

    src[:, 0:leaf_dev] = m[...]
    mid = first.shape[0]
    a, b = first[...].astype(f32), second[...].astype(f32)
    low, high = jnp.where(is_odd, b, a), jnp.where(is_odd, a, b)
    low_lane = lax.broadcasted_iota(jnp.int32, (mid, leaf_dev), 1) < half
    upper = jnp.where(low_lane, low, pltpu.roll(high, half, 1))
    lower = jnp.where(low_lane, pltpu.roll(low, half, 1), high)
    src[0:mid, leaf_dev:] = upper.astype(bf16)
    src[mid:, leaf_dev:] = lower.astype(bf16)
    place_of = lax.broadcasted_iota(jnp.int32, (window, 128), 0).astype(f32).astype(bf16)

    def chosen(ref, group, at):
        row = ref[pl.ds(slot_of(group, at), 1), :].astype(f32).astype(bf16)
        return jnp.where(place_of == row, jnp.ones((), bf16), jnp.zeros((), bf16))

    def picks(source, ref, group, held, last, chunk):
        count = source.shape[0] // kcount
        for pair in range(GROUP // 2):
            at = 2 * pair
            both = jnp.concatenate([chosen(ref, group, at), chosen(ref, group, at + 1)], axis=1)
            for begin in range(0, count, chunk):
                end = begin + chunk
                end_row = end * KM if end < count else source.shape[0]
                picked = nn(source[begin * KM : end_row, :], both)
                for c in range(chunk):
                    rows = picked[c * KM : (c + 1) * KM]
                    lane = (begin + c) * 128
                    held[at * KM : (at + 2) * KM, lane : lane + 128] = jnp.concatenate(
                        [rows[:, 0:128], rows[:, 128:]], axis=0
                    ).astype(bf16)
            rows = picked[chunk * KM :]
            for i in range(2):
                for c in range(count):
                    last[at + i : at + i + 1, c * 128 : (c + 1) * 128] = rows[c : c + 1, i * 128 : (i + 1) * 128]
        held[GROUP * KM :, :] = last[...].astype(bf16)

    def pick_leaves(group, held, last):
        picks(src, idx, group, held, last, CHUNK)

    def pick_parents(group, held_c, last_c):
        picks(srcc, idxc, group, held_c, last_c, srcc.shape[0] // kcount)

    def pick_group(group, held, last, held_c, last_c):
        pick_leaves(group, held, last)
        pick_parents(group, held_c, last_c)

    def gradients(group, held, held_c):
        blocks[group, :, 0:tight] = nt(be[...], held[...])
        blocks[steps + group, :, 0:tight] = nt(bf[...], held_c[...])

    def fields(group, held, held_c):
        near[...] += nn(lops[group][:, 0:tight], held[...])
        far[...] += nn(cops[group][:, 0:tight], held_c[...])

    for ref in (near, far, even_last, odd_last, even_c_last, odd_c_last):
        ref[...] = jnp.zeros_like(ref)
    evens, odds = (even, even_last, even_c, even_c_last), (odd, odd_last, odd_c, odd_c_last)
    pick_leaves(0, even, even_last)
    lay_wide(jnp.concatenate([upper, lower], axis=0), wide)
    srcc[:, 0:128] = cc[...]
    srcc[:, 128:] = tightened(upward(up[...], wide, sums, pool))
    pick_parents(0, even_c, even_c_last)

    def two_groups(i, carry):
        group = 2 * i + 1
        gradients(group - 1, even, even_c)
        pick_group(group, *odds)
        fields(group - 1, even, even_c)
        gradients(group, odd, odd_c)
        pick_group(group + 1, *evens)
        fields(group, odd, odd_c)
        return carry

    lax.fori_loop(0, steps // 2 - 1, two_groups, 0)
    pick_group(steps - 1, *odds)
    gradients(steps - 2, even, even_c)
    gradients(steps - 1, odd, odd_c)
    flat[...] = jnp.zeros_like(flat)
    main = GROUP * KM
    for turn in range(-(-kcount // FOUR)):
        several = jnp.concatenate([blocks[:, turn * FOUR + k, :] for k in range(FOUR)], axis=0)
        across = several.T
        for tile in range(GROUP // 2):
            at = 2 * tile
            body = jnp.concatenate([across[a * KM : (a + 1) * KM] for a in (at, at + 1)], axis=1)
            rest = jnp.concatenate([across[main + a : main + a + 1] for a in (at, at + 1)], axis=1)
            rows = pl.ds(turn * FOUR * kcount + tile, kcount, stride=FOUR)
            flat[rows, :] = jnp.concatenate([body, rest], axis=0)
    fields(steps - 2, even, even_c)
    fields(steps - 1, odd, odd_c)
    if len(g_out.shape) == 2:
        g_out[...] = flat[...].astype(bf16)
    else:
        for d in range(g_out.shape[0]):
            g_out[d] = flat[d * g_out.shape[1] : (d + 1) * g_out.shape[1], :].astype(bf16)


def potential_kernel(near, far, down, base, inside, out, order, field, total):
    leaf_dev = near.shape[1] // out.shape[0]
    lanes = OCT * 128
    copies = jnp.where(
        lax.broadcasted_iota(jnp.int32, (128, lanes), 1) // OCT
        == lax.broadcasted_iota(jnp.int32, (128, lanes), 0),
        1.0,
        0.0,
    ).astype(bf16)
    for at in range(far.shape[1] // 128):
        parent = nn(far[:, at * 128 : (at + 1) * 128].astype(bf16), copies).astype(bf16)
        child = nn(down[...], by_octant(parent))
        columns = slice(at * lanes, (at + 1) * lanes)
        expansion = (near[:, columns] + child).astype(bf16)
        for c in range(OCT):
            field[c * KP : (c + 1) * KP, :] = expansion[:, c * leaf_dev : (c + 1) * leaf_dev]
        for c in range(OCT):
            row = at * OCT + c
            per_atom = nn(field[c * KP : (c + 1) * KP, :], inside[...])
            total[row : row + 1, :] = jnp.sum(base[...] * per_atom, axis=0, keepdims=True)
    out[...] = total[...].astype(bf16)
    order[...] = turned_order()


def turned_order():
    size = FOUR * 128
    row = lax.broadcasted_iota(jnp.int32, (size, size), 0)
    k, level, group, at = row // 16 % FOUR, row // GROUP % 2, row % GROUP, row // 64
    wanted = k * 128 + level * 64 + slot_of(group, at)
    return jnp.where(lax.broadcasted_iota(jnp.int32, (size, size), 1) == wanted, 1.0, 0.0).astype(bf16)


def reduce_kernel(parts, after, order, out, total, laid):
    summed = parts[0].astype(f32)
    for d in range(1, parts.shape[0]):
        summed = summed + parts[d].astype(f32)
    total[...] = summed
    count = summed.shape[0] // FOUR
    tiles = [total[pl.ds(tile, count, stride=FOUR), :] for tile in range(FOUR)]
    turned = nn(jnp.concatenate(tiles, axis=1).astype(bf16), order[...])
    for k in range(FOUR):
        laid[pl.ds(k, count, stride=FOUR), :] = turned[:, k * 128 : (k + 1) * 128]
    for d in range(out.shape[0]):
        out[d] = laid[...].astype(bf16)


def unpack_kernel(whole, leaf_out, coarse_out, flat):
    kcount, jcount, slots = leaf_out.shape
    if len(whole.shape) == 2:
        flat[...] = whole[...].astype(f32)
    else:
        for d in range(whole.shape[0]):
            flat[d * whole.shape[1] : (d + 1) * whole.shape[1], :] = whole[d].astype(f32)
    for k in range(kcount):
        row = flat[pl.ds(k // FOUR * FOUR * jcount + k % FOUR, jcount, stride=FOUR), :]
        leaf_out[k] = row[:, 0:slots]
        coarse_out[k] = pltpu.roll(row, slots, 1)[:, 0:slots]


def mixing_kernel(whole, mix, charges, out, mixed):
    part = out.shape[0]
    me = lax.axis_index("chan")
    mixed[...] = lax.dot_general(
        mix[...], whole[...], (((0,), (0,)), ((), ())), preferred_element_type=f32
    )
    out[...] = (charges[...].astype(f32) + mixed[pl.ds(me * part, part), :]).astype(bf16)


def call(kernel, outs, scratch, flops=10**8, moved=10**6, limit=VMEM_BYTES, **kw):
    return pl.pallas_call(
        kernel,
        out_shape=outs,
        scratch_shapes=scratch,
        compiler_params=pltpu.CompilerParams(vmem_limit_bytes=limit),
        cost_estimate=pl.CostEstimate(flops=flops, bytes_accessed=moved, transcendentals=0),
        **kw,
    )


def from_chan(block):
    count = lax.axis_size("chan")

    def swap(part, d):
        return lax.ppermute(part, "chan", [(i, i ^ d) for i in range(count)])

    cross = swap(block, 2)
    return [swap(block, 1), cross, swap(cross, 1)]


def local(
    charges, basis, atom_leaf, leaf_lists, coarse_lists, up_ops, down_ops, leaf_ops, coarse_ops, mix, cotangent
):
    part, atoms = charges.shape
    kcount = basis.shape[0]
    slots, leaf_dev = leaf_lists.shape
    rows = part * kcount
    coarse_rows = rows // OCT
    steps = slots // GROUP
    cells = lax.axis_size("cells")
    devices = cells * lax.axis_size("chan")
    leaf = atom_leaf.reshape(1, atoms)
    shape = jax.ShapeDtypeStruct
    far_off = pl.BlockSpec(memory_space=pltpu.HBM)
    near_by = pl.BlockSpec(memory_space=pltpu.VMEM)
    like = lambda a: pltpu.VMEM(a.shape, a.dtype)
    stay = lambda *arrays: [pltpu.with_memory_space_constraint(a, pltpu.HBM) for a in arrays]
    wide = part * leaf_dev

    held = (
        cotangent,
        mix,
        jnp.swapaxes(up_ops, 0, 1),
        jnp.swapaxes(down_ops, 0, 1),
        leaf_ops,
        coarse_ops,
        leaf_lists,
        coarse_lists.T,
    )
    m, first, second, base, inside, pool, charges_near, *held = call(
        moments_kernel,
        (
            shape((rows, leaf_dev), bf16),
            shape((rows // 2, leaf_dev), bf16),
            shape((rows // 2, leaf_dev), bf16),
            shape((KP, atoms), f32),
            shape((leaf_dev, atoms), bf16),
            shape((OCT * 128, 128), bf16),
            shape(charges.shape, bf16),
            *[shape(a.shape, a.dtype) for a in held],
        ),
        [like(basis), like(leaf), pltpu.VMEM((rows, atoms), bf16), pltpu.SemaphoreType.DMA((3 + MORE,))],
        in_specs=[far_off] * (3 + MORE),
    )(*stay(charges, basis, leaf, *held))
    inner = [(i, i + 1) for i in range(1, cells - 1, 2)]
    outer = [(i, i + 1) for i in range(0, cells - 1, 2)]
    first = lax.ppermute(first, "cells", inner + [(b, a) for a, b in inner])
    second = lax.ppermute(second, "cells", outer + [(b, a) for a, b in outer])
    own, mix_near, *prepared = held
    cot = from_chan(own)

    wide_ops = shape((KP, OCT * KP), bf16)
    group_ops = shape((steps, KP, GROUP * KP), bf16)
    cc, up, down, back_ops, lops, cops, idx, idxc = call(
        prepare_kernel,
        (
            shape((coarse_rows, 128), bf16),
            wide_ops,
            wide_ops,
            wide_ops,
            group_ops,
            group_ops,
            shape((slots, 128), jnp.int32),
            shape((slots, 128), jnp.int32),
        ),
        [
            pltpu.VMEM((KP, wide), bf16),
            pltpu.VMEM((2, OCT, KP, 128), f32),
            pltpu.VMEM((kcount, KP, 128), f32),
            pltpu.VMEM((KP, slots, KP), f32),
            pltpu.VMEM((128, OCT * 128), bf16),
        ],
        flops=10**8,
    )(*prepared, m, pool)
    be, bf = call(
        back_kernel,
        (shape((KP, wide), bf16), shape((KP, wide // OCT), bf16)),
        [
            pltpu.VMEM((rows, atoms), bf16),
            pltpu.VMEM((mix.shape[0], atoms), bf16),
            pltpu.VMEM((128, OCT * 128), bf16),
        ],
    )(own, *cot, mix_near, base, inside, pool, back_ops)

    flat_rows = -(-(-(-kcount // FOUR) * FOUR * kcount) // 256) * 256
    fits = flat_rows % (8 * devices) == 0
    laid = (devices, flat_rows // devices, 128) if fits else (flat_rows, 128)
    near, far, grads = call(
        functools.partial(grads_kernel, kcount=kcount),
        (shape((KP, wide), f32), shape((KP, wide // OCT), f32), shape(laid, bf16)),
        [
            pltpu.VMEM((rows, 2 * leaf_dev), bf16),
            pltpu.VMEM((coarse_rows, 256), bf16),
            pltpu.VMEM((KP, wide), bf16),
            pltpu.VMEM((GROUP * KM + 16, wide), bf16),
            pltpu.VMEM((GROUP * KM + 16, wide), bf16),
            pltpu.VMEM((GROUP * KM + 16, wide // OCT), bf16),
            pltpu.VMEM((GROUP * KM + 16, wide // OCT), bf16),
            pltpu.VMEM((16, wide), f32),
            pltpu.VMEM((16, wide), f32),
            pltpu.VMEM((16, wide // OCT), f32),
            pltpu.VMEM((16, wide // OCT), f32),
            pltpu.VMEM((128, OCT * 128), bf16),
            pltpu.VMEM((2 * steps, KP, GROUP * KP), f32),
            pltpu.VMEM((flat_rows, 128), f32),
        ],
    )(m, first, second, cc, be, bf, up, idx, idxc, lops, cops, pool)
    potential, order = call(
        potential_kernel,
        (shape((part, atoms), bf16), shape((FOUR * 128, FOUR * 128), bf16)),
        [pltpu.VMEM((OCT * KP, leaf_dev), bf16), pltpu.VMEM((part, atoms), f32)],
    )(near, far, down, base, inside)

    axes = ("cells", "chan")
    if fits:
        parts = lax.all_to_all(grads, axes, 0, 0)
        spread_out = call(
            reduce_kernel,
            shape(laid, bf16),
            [pltpu.VMEM(laid[1:], f32), pltpu.VMEM(laid[1:], f32)],
            in_specs=[near_by, pl.BlockSpec(memory_space=pl.ANY), near_by],
        )(parts, potential, order)
        whole = lax.all_to_all(spread_out, axes, 0, 0)
    else:
        split = -(-flat_rows // devices) * devices
        pieces = jnp.pad(grads, ((0, split - flat_rows), (0, 0))).reshape(devices, -1, 128)
        parts = lax.all_to_all(pieces, axes, 0, 0)
        mine = jnp.sum(parts.astype(f32), axis=0).astype(bf16)
        whole = lax.all_gather(mine, axes).reshape(split, 128)[:flat_rows]
        whole = whole.reshape(flat_rows // FOUR, FOUR, 2, FOUR, 2, GROUP)
        whole = jnp.transpose(whole, (0, 3, 4, 1, 2, 5)).reshape(flat_rows, 128)
    grad_shape = shape((kcount, kcount, slots), f32)
    grad_leaf, grad_coarse = call(
        unpack_kernel, (grad_shape, grad_shape), [pltpu.VMEM((flat_rows, 128), f32)]
    )(whole)

    refined = call(
        mixing_kernel,
        shape((part, atoms), bf16),
        [pltpu.VMEM((mix.shape[0], atoms), f32)],
    )(lax.all_gather(potential, "chan", axis=0, tiled=True), mix_near, charges_near)
    return refined, grad_leaf, grad_coarse


def solution(mesh):
    placed = (
        P("chan", "cells"),
        P(None, "cells"),
        P("cells"),
        P(None, "cells"),
        P(None, "cells"),
        P(),
        P(),
        P(),
        P(),
        P(),
        P("chan", "cells"),
    )
    return jax.shard_map(
        local, mesh=mesh, in_specs=placed, out_specs=(P("chan", "cells"), P(), P()), check_vma=False
    )
```

```python
import functools

import jax
import jax.numpy as jnp
from jax import lax
from jax.experimental import pallas as pl
from jax.experimental.pallas import tpu as pltpu
from jax.sharding import PartitionSpec as P

KP = 32
GROUP = 8
KM = 24
CHUNK = 16
FOUR = 4
OCT = 8
MORE = 8
VMEM_BYTES = 24 * 1024 * 1024
f32 = jnp.float32
bf16 = jnp.bfloat16


def nt(a, b):
    return lax.dot_general(a, b, (((1,), (1,)), ((), ())), preferred_element_type=f32)


def nn(a, b):
    return jnp.dot(a, b, preferred_element_type=f32)


def member(leaf_row, leaf_dev):
    shape = (leaf_dev, leaf_row.shape[1])
    return jnp.where(lax.broadcasted_iota(jnp.int32, shape, 0) == leaf_row, 1.0, 0.0).astype(bf16)


def spread(base, values, scaled):
    wide = values.astype(f32)
    count = values.shape[0]
    for c in range(0, count, 2):
        pair = [base[0:KM, :] * wide[c + i : c + i + 1, :] for i in range(2)]
        scaled[c * KM : (c + 2) * KM, :] = jnp.concatenate(pair, axis=0).astype(bf16)
    scaled[count * KM :, :] = (base[KM : KM + 1, :] * wide).astype(bf16)


def lay_wide(rows, out):
    count = rows.shape[0] // (KM + 1)
    lanes = rows.shape[1]
    top = lax.broadcasted_iota(jnp.int32, (KP - KM, lanes), 0) == 0
    for c in range(count):
        last = jnp.where(top, rows[count * KM + c : count * KM + c + 1, :], 0.0)
        block = jnp.concatenate([rows[c * KM : (c + 1) * KM, :], last], axis=0)
        out[:, c * lanes : (c + 1) * lanes] = block.astype(bf16)


def fetch(pairs, sems):
    copies = [pltpu.make_async_copy(src, dst, sems.at[i]) for i, (src, dst) in enumerate(pairs)]
    for copy in copies:
        copy.start()
    return copies


def pooling(rows, cols):
    return jnp.where(
        lax.broadcasted_iota(jnp.int32, (rows, cols), 0) // OCT
        == lax.broadcasted_iota(jnp.int32, (rows, cols), 1),
        1.0,
        0.0,
    ).astype(bf16)


def by_octant(values):
    octant = lax.broadcasted_iota(jnp.int32, (1, values.shape[1]), 1) % OCT
    return jnp.concatenate(
        [values * jnp.where(octant == o, 1.0, 0.0).astype(values.dtype) for o in range(OCT)], axis=0
    )


def upward(ops, wide_ref, sums, pool):
    lanes = OCT * 128
    for part in range(wide_ref.shape[1] // lanes):
        spaced = by_octant(wide_ref[:, part * lanes : (part + 1) * lanes])
        sums[part * KP : (part + 1) * KP, :] = nn(ops, spaced).astype(bf16)
    return nn(sums[...], pool[...])


def tightened(rows):
    count = rows.shape[0] // KP
    whole = [rows[c * KP : c * KP + KM] for c in range(count)]
    last = [rows[c * KP + KM : c * KP + KM + 1] for c in range(count)]
    return jnp.concatenate(whole + last, axis=0).astype(bf16)


def moments_kernel(charges_hbm, basis_hbm, leaf_hbm, *rest):
    more = rest[:MORE]
    m_out, first_out, second_out, base_out, inside_out, pool_out, charges = rest[MORE : MORE + 7]
    held = rest[MORE + 7 : 2 * MORE + 7]
    basis, leaf, scaled, sems = rest[2 * MORE + 7 :]
    leaf_dev = m_out.shape[1]
    half = leaf_dev // 2
    cell = lax.axis_index("cells")
    copies = fetch(
        [(charges_hbm, charges), (basis_hbm, basis), (leaf_hbm, leaf), *zip(more, held)], sems
    )
    kcount = basis.shape[0]
    base_out[...] = jnp.zeros_like(base_out)
    pool_out[...] = pooling(*pool_out.shape)
    for copy in copies[:3]:
        copy.wait()
    base_out[0:kcount, :] = basis[...]
    inside_out[...] = member(leaf[...] - cell * leaf_dev, leaf_dev)
    spread(base_out, charges[...], scaled)
    m = nt(scaled[...], inside_out[...])
    m_out[...] = m.astype(bf16)
    rows = m.shape[0] // 2
    upper, lower = m[:rows], m[rows:]
    low_lane = lax.broadcasted_iota(jnp.int32, (rows, leaf_dev), 1) < half
    hi = jnp.where(low_lane, pltpu.roll(upper, half, 1), lower).astype(bf16)
    lo = jnp.where(low_lane, upper, pltpu.roll(lower, half, 1)).astype(bf16)
    odd = lax.rem(cell, 2)
    first_out[...] = jnp.where(odd == 1, hi, lo)
    second_out[...] = jnp.where(odd == 1, lo, hi)
    for copy in copies[3:]:
        copy.wait()


def slot_of(group, at):
    return at * GROUP + group


def slot_ops(ops, padded, turned, out):
    kcount, jcount, slots = ops.shape
    turned[...] = jnp.zeros_like(turned)
    padded[...] = jnp.zeros_like(padded)
    for k in range(kcount):
        padded[k, 0:jcount, 0:slots] = ops[k].astype(f32)
        turned[k, :, :] = padded[k].T[0:slots]
    for group in range(out.shape[0]):
        held = [turned[:, slot_of(group, at), :] for at in range(GROUP)]
        pieces = [a[:, 0:KM] for a in held] + [a[:, KM : KM + 1] for a in held]
        pieces.append(jnp.zeros((KP, GROUP * KP - GROUP * (KM + 1)), f32))
        out[group] = jnp.concatenate(pieces, axis=1).astype(bf16)


def prepare_kernel(
    up,
    down,
    lops,
    cops,
    ll,
    cl,
    m,
    pool,
    cc_out,
    up_out,
    down_out,
    back_out,
    lops_out,
    cops_out,
    idx,
    idxc,
    wide,
    stack,
    padded,
    turned,
    sums,
):
    leaf_dev = m.shape[1]
    half = leaf_dev // 2
    kcount = up.shape[0]
    coarse_dev, slots = cl.shape
    cell = lax.axis_index("cells")
    lay_wide(m[...].astype(f32), wide)
    stack[...] = jnp.zeros_like(stack)
    for k in range(kcount):
        stack[0, :, k, 0:kcount] = up[k].astype(f32)
        stack[1, :, k, 0:kcount] = down[k].astype(f32)

    def side_by_side(pieces):
        return jnp.concatenate(pieces, axis=1).astype(bf16)

    up_out[...] = side_by_side([stack[0, o, :, 0:KP] for o in range(OCT)])
    down_out[...] = side_by_side([stack[1, o, :, 0:KP] for o in range(OCT)])
    back_out[...] = side_by_side([stack[1, o].T[0:KP, :] for o in range(OCT)])
    cc_out[...] = tightened(upward(up_out[...], wide, sums, pool))

    slot_ops(lops, padded, turned, lops_out)
    slot_ops(cops, padded, turned, cops_out)
    rel = ll[...] - cell * leaf_dev
    place = jnp.where(rel < 0, rel + leaf_dev + half, jnp.where(rel < leaf_dev, rel, rel + half))
    idx[0:slots, :] = jnp.where(ll[...] < 0, -1, place)
    idx[slots:, :] = jnp.full_like(idx[slots:, :], -1)
    crel = cl[...] - cell * coarse_dev
    side = coarse_dev // 2
    cplace = jnp.where(crel < 0, crel + 128 + side, jnp.where(crel < coarse_dev, crel, crel + 128 - side))
    cplace = jnp.where(cl[...] < 0, -1, cplace).astype(f32).astype(bf16)
    copied = jnp.where(
        lax.broadcasted_iota(jnp.int32, (coarse_dev, 128), 0)
        == lax.broadcasted_iota(jnp.int32, (coarse_dev, 128), 1) % coarse_dev,
        1.0,
        0.0,
    ).astype(bf16)
    spot = lax.dot_general(cplace, copied, (((0,), (0,)), ((), ())), preferred_element_type=f32)
    spot = spot.astype(jnp.int32)
    start = lax.broadcasted_iota(jnp.int32, (slots, 128), 1) // coarse_dev * coarse_dev
    idxc[0:slots, :] = jnp.where(spot < 0, -1, spot + start)
    idxc[slots:, :] = jnp.full_like(idxc[slots:, :], -1)


def back_kernel(own, core, cross, other, mix, base, inside, pool, back_ops, be_out, bf_out, scaled, gathered, sums):
    part = own.shape[0]
    me = lax.axis_index("chan")
    gathered[pl.ds(me * part, part), :] = own[...]
    gathered[pl.ds((me ^ 1) * part, part), :] = core[...]
    gathered[pl.ds((me ^ 2) * part, part), :] = cross[...]
    gathered[pl.ds((me ^ 3) * part, part), :] = other[...]
    potential = nn(mix[pl.ds(me * part, part), :], gathered[...]).astype(bf16)
    spread(base, potential, scaled)
    lay_wide(nt(scaled[...], inside[...]), be_out)
    far = upward(back_ops[...], be_out, sums, pool).astype(bf16)
    for at in range(far.shape[0] // KP):
        bf_out[:, at * 128 : (at + 1) * 128] = far[at * KP : (at + 1) * KP, :]


def grads_kernel(
    m,
    first,
    second,
    cc,
    be,
    bf,
    up,
    idx,
    idxc,
    lops,
    cops,
    pool,
    near,
    far,
    g_out,
    src,
    srcc,
    wide,
    even,
    odd,
    even_c,
    odd_c,
    even_last,
    odd_last,
    even_c_last,
    odd_c_last,
    sums,
    blocks,
    flat,
    *,
    kcount,
):
    leaf_dev = m.shape[1]
    half = leaf_dev // 2
    window = 2 * leaf_dev
    channels = m.shape[0] // kcount
    steps = lops.shape[0]
    tight = even.shape[0]
    is_odd = lax.rem(lax.axis_index("cells"), 2) == 1

    src[:, 0:leaf_dev] = m[...]
    mid = first.shape[0]
    a, b = first[...].astype(f32), second[...].astype(f32)
    low, high = jnp.where(is_odd, b, a), jnp.where(is_odd, a, b)
    low_lane = lax.broadcasted_iota(jnp.int32, (mid, leaf_dev), 1) < half
    upper = jnp.where(low_lane, low, pltpu.roll(high, half, 1))
    lower = jnp.where(low_lane, pltpu.roll(low, half, 1), high)
    src[0:mid, leaf_dev:] = upper.astype(bf16)
    src[mid:, leaf_dev:] = lower.astype(bf16)
    place_of = lax.broadcasted_iota(jnp.int32, (window, 128), 0).astype(f32).astype(bf16)

    def chosen(ref, group, at):
        row = ref[pl.ds(slot_of(group, at), 1), :].astype(f32).astype(bf16)
        return jnp.where(place_of == row, jnp.ones((), bf16), jnp.zeros((), bf16))

    def picks(source, ref, group, held, last, chunk):
        count = source.shape[0] // kcount
        for pair in range(GROUP // 2):
            at = 2 * pair
            both = jnp.concatenate([chosen(ref, group, at), chosen(ref, group, at + 1)], axis=1)
            for begin in range(0, count, chunk):
                end = begin + chunk
                end_row = end * KM if end < count else source.shape[0]
                picked = nn(source[begin * KM : end_row, :], both)
                for c in range(chunk):
                    rows = picked[c * KM : (c + 1) * KM]
                    lane = (begin + c) * 128
                    held[at * KM : (at + 2) * KM, lane : lane + 128] = jnp.concatenate(
                        [rows[:, 0:128], rows[:, 128:]], axis=0
                    ).astype(bf16)
            rows = picked[chunk * KM :]
            for i in range(2):
                for c in range(count):
                    last[at + i : at + i + 1, c * 128 : (c + 1) * 128] = rows[c : c + 1, i * 128 : (i + 1) * 128]
        held[GROUP * KM :, :] = last[...].astype(bf16)

    def pick_leaves(group, held, last):
        picks(src, idx, group, held, last, CHUNK)

    def pick_parents(group, held_c, last_c):
        picks(srcc, idxc, group, held_c, last_c, srcc.shape[0] // kcount)

    def pick_group(group, held, last, held_c, last_c):
        pick_leaves(group, held, last)
        pick_parents(group, held_c, last_c)

    def gradients(group, held, held_c):
        blocks[group, :, 0:tight] = nt(be[...], held[...])
        blocks[steps + group, :, 0:tight] = nt(bf[...], held_c[...])

    def fields(group, held, held_c):
        near[...] += nn(lops[group][:, 0:tight], held[...])
        far[...] += nn(cops[group][:, 0:tight], held_c[...])

    for ref in (near, far, even_last, odd_last, even_c_last, odd_c_last):
        ref[...] = jnp.zeros_like(ref)
    evens, odds = (even, even_last, even_c, even_c_last), (odd, odd_last, odd_c, odd_c_last)
    pick_leaves(0, even, even_last)
    lay_wide(jnp.concatenate([upper, lower], axis=0), wide)
    srcc[:, 0:128] = cc[...]
    srcc[:, 128:] = tightened(upward(up[...], wide, sums, pool))
    pick_parents(0, even_c, even_c_last)

    def two_groups(i, carry):
        group = 2 * i + 1
        gradients(group - 1, even, even_c)
        pick_group(group, *odds)
        fields(group - 1, even, even_c)
        gradients(group, odd, odd_c)
        pick_group(group + 1, *evens)
        fields(group, odd, odd_c)
        return carry

    lax.fori_loop(0, steps // 2 - 1, two_groups, 0)
    pick_group(steps - 1, *odds)
    gradients(steps - 2, even, even_c)
    gradients(steps - 1, odd, odd_c)
    flat[...] = jnp.zeros_like(flat)
    main = GROUP * KM
    for turn in range(-(-kcount // FOUR)):
        several = jnp.concatenate([blocks[:, turn * FOUR + k, :] for k in range(FOUR)], axis=0)
        across = several.T
        for tile in range(GROUP // 2):
            at = 2 * tile
            body = jnp.concatenate([across[a * KM : (a + 1) * KM] for a in (at, at + 1)], axis=1)
            rest = jnp.concatenate([across[main + a : main + a + 1] for a in (at, at + 1)], axis=1)
            rows = pl.ds(turn * FOUR * kcount + tile, kcount, stride=FOUR)
            flat[rows, :] = jnp.concatenate([body, rest], axis=0)
    fields(steps - 2, even, even_c)
    fields(steps - 1, odd, odd_c)
    if len(g_out.shape) == 2:
        g_out[...] = flat[...].astype(bf16)
    else:
        for d in range(g_out.shape[0]):
            g_out[d] = flat[d * g_out.shape[1] : (d + 1) * g_out.shape[1], :].astype(bf16)


def potential_kernel(near, far, down, base, inside, out, order, field, total):
    leaf_dev = near.shape[1] // out.shape[0]
    lanes = OCT * 128
    copies = jnp.where(
        lax.broadcasted_iota(jnp.int32, (128, lanes), 1) // OCT
        == lax.broadcasted_iota(jnp.int32, (128, lanes), 0),
        1.0,
        0.0,
    ).astype(bf16)
    for at in range(far.shape[1] // 128):
        parent = nn(far[:, at * 128 : (at + 1) * 128].astype(bf16), copies).astype(bf16)
        child = nn(down[...], by_octant(parent))
        columns = slice(at * lanes, (at + 1) * lanes)
        expansion = (near[:, columns] + child).astype(bf16)
        for c in range(OCT):
            field[c * KP : (c + 1) * KP, :] = expansion[:, c * leaf_dev : (c + 1) * leaf_dev]
        for c in range(OCT):
            row = at * OCT + c
            per_atom = nn(field[c * KP : (c + 1) * KP, :], inside[...])
            total[row : row + 1, :] = jnp.sum(base[...] * per_atom, axis=0, keepdims=True)
    out[...] = total[...].astype(bf16)
    order[...] = turned_order()


def turned_order():
    size = FOUR * 128
    row = lax.broadcasted_iota(jnp.int32, (size, size), 0)
    k, level, group, at = row // 16 % FOUR, row // GROUP % 2, row % GROUP, row // 64
    wanted = k * 128 + level * 64 + slot_of(group, at)
    return jnp.where(lax.broadcasted_iota(jnp.int32, (size, size), 1) == wanted, 1.0, 0.0).astype(bf16)


def reduce_kernel(parts, after, order, out, total, laid):
    summed = parts[0].astype(f32)
    for d in range(1, parts.shape[0]):
        summed = summed + parts[d].astype(f32)
    total[0 : summed.shape[0], :] = summed
    count = summed.shape[0] // FOUR
    tiles = [total[pl.ds(tile, count, stride=FOUR), :] for tile in range(FOUR)]
    turned = nn(jnp.concatenate(tiles, axis=1).astype(bf16), order[...])
    for k in range(FOUR):
        laid[pl.ds(k, count, stride=FOUR), :] = turned[:, k * 128 : (k + 1) * 128]
    for d in range(out.shape[0]):
        out[d] = laid[0 : summed.shape[0], :].astype(bf16)


def unpack_kernel(whole, leaf_out, coarse_out, flat):
    kcount, jcount, slots = leaf_out.shape
    if len(whole.shape) == 2:
        flat[...] = whole[...].astype(f32)
    else:
        for d in range(whole.shape[0]):
            flat[d * whole.shape[1] : (d + 1) * whole.shape[1], :] = whole[d].astype(f32)
    for k in range(kcount):
        row = flat[pl.ds(k // FOUR * FOUR * jcount + k % FOUR, jcount, stride=FOUR), :]
        leaf_out[k] = row[:, 0:slots]
        coarse_out[k] = pltpu.roll(row, slots, 1)[:, 0:slots]


def mixing_kernel(whole, mix, charges, out, mixed):
    part = out.shape[0]
    me = lax.axis_index("chan")
    mixed[...] = lax.dot_general(
        mix[...], whole[...], (((0,), (0,)), ((), ())), preferred_element_type=f32
    )
    out[...] = (charges[...].astype(f32) + mixed[pl.ds(me * part, part), :]).astype(bf16)


def call(kernel, outs, scratch, flops=10**8, moved=10**6, limit=VMEM_BYTES, **kw):
    return pl.pallas_call(
        kernel,
        out_shape=outs,
        scratch_shapes=scratch,
        compiler_params=pltpu.CompilerParams(vmem_limit_bytes=limit),
        cost_estimate=pl.CostEstimate(flops=flops, bytes_accessed=moved, transcendentals=0),
        **kw,
    )


def from_chan(block):
    count = lax.axis_size("chan")

    def swap(part, d):
        return lax.ppermute(part, "chan", [(i, i ^ d) for i in range(count)])

    cross = swap(block, 2)
    return [swap(block, 1), cross, swap(cross, 1)]


def local(
    charges, basis, atom_leaf, leaf_lists, coarse_lists, up_ops, down_ops, leaf_ops, coarse_ops, mix, cotangent
):
    part, atoms = charges.shape
    kcount = basis.shape[0]
    slots, leaf_dev = leaf_lists.shape
    rows = part * kcount
    coarse_rows = rows // OCT
    steps = slots // GROUP
    cells = lax.axis_size("cells")
    devices = cells * lax.axis_size("chan")
    leaf = atom_leaf.reshape(1, atoms)
    shape = jax.ShapeDtypeStruct
    far_off = pl.BlockSpec(memory_space=pltpu.HBM)
    near_by = pl.BlockSpec(memory_space=pltpu.VMEM)
    like = lambda a: pltpu.VMEM(a.shape, a.dtype)
    stay = lambda *arrays: [pltpu.with_memory_space_constraint(a, pltpu.HBM) for a in arrays]
    wide = part * leaf_dev

    held = (
        cotangent,
        mix,
        jnp.swapaxes(up_ops, 0, 1),
        jnp.swapaxes(down_ops, 0, 1),
        leaf_ops,
        coarse_ops,
        leaf_lists,
        coarse_lists.T,
    )
    m, first, second, base, inside, pool, charges_near, *held = call(
        moments_kernel,
        (
            shape((rows, leaf_dev), bf16),
            shape((rows // 2, leaf_dev), bf16),
            shape((rows // 2, leaf_dev), bf16),
            shape((KP, atoms), f32),
            shape((leaf_dev, atoms), bf16),
            shape((OCT * 128, 128), bf16),
            shape(charges.shape, bf16),
            *[shape(a.shape, a.dtype) for a in held],
        ),
        [like(basis), like(leaf), pltpu.VMEM((rows, atoms), bf16), pltpu.SemaphoreType.DMA((3 + MORE,))],
        in_specs=[far_off] * (3 + MORE),
    )(*stay(charges, basis, leaf, *held))
    inner = [(i, i + 1) for i in range(1, cells - 1, 2)]
    outer = [(i, i + 1) for i in range(0, cells - 1, 2)]
    first = lax.ppermute(first, "cells", inner + [(b, a) for a, b in inner])
    second = lax.ppermute(second, "cells", outer + [(b, a) for a, b in outer])
    own, mix_near, *prepared = held
    cot = from_chan(own)

    wide_ops = shape((KP, OCT * KP), bf16)
    group_ops = shape((steps, KP, GROUP * KP), bf16)
    cc, up, down, back_ops, lops, cops, idx, idxc = call(
        prepare_kernel,
        (
            shape((coarse_rows, 128), bf16),
            wide_ops,
            wide_ops,
            wide_ops,
            group_ops,
            group_ops,
            shape((slots + 8, 128), jnp.int32),
            shape((slots + 8, 128), jnp.int32),
        ),
        [
            pltpu.VMEM((KP, wide), bf16),
            pltpu.VMEM((2, OCT, KP, 128), f32),
            pltpu.VMEM((kcount, KP, 128), f32),
            pltpu.VMEM((KP, slots, KP), f32),
            pltpu.VMEM((128, OCT * 128), bf16),
        ],
        flops=10**8,
    )(*prepared, m, pool)
    be, bf = call(
        back_kernel,
        (shape((KP, wide), bf16), shape((KP, wide // OCT), bf16)),
        [
            pltpu.VMEM((rows, atoms), bf16),
            pltpu.VMEM((mix.shape[0], atoms), bf16),
            pltpu.VMEM((128, OCT * 128), bf16),
        ],
    )(own, *cot, mix_near, base, inside, pool, back_ops)

    flat_rows = -(-(-(-kcount // FOUR) * FOUR * kcount) // 256) * 256
    fits = flat_rows % (8 * devices) == 0
    laid = (devices, flat_rows // devices, 128) if fits else (flat_rows, 128)
    near, far, grads = call(
        functools.partial(grads_kernel, kcount=kcount),
        (shape((KP, wide), f32), shape((KP, wide // OCT), f32), shape(laid, bf16)),
        [
            pltpu.VMEM((rows, 2 * leaf_dev), bf16),
            pltpu.VMEM((coarse_rows, 256), bf16),
            pltpu.VMEM((KP, wide), bf16),
            pltpu.VMEM((GROUP * KM + 16, wide), bf16),
            pltpu.VMEM((GROUP * KM + 16, wide), bf16),
            pltpu.VMEM((GROUP * KM + 16, wide // OCT), bf16),
            pltpu.VMEM((GROUP * KM + 16, wide // OCT), bf16),
            pltpu.VMEM((16, wide), f32),
            pltpu.VMEM((16, wide), f32),
            pltpu.VMEM((16, wide // OCT), f32),
            pltpu.VMEM((16, wide // OCT), f32),
            pltpu.VMEM((128, OCT * 128), bf16),
            pltpu.VMEM((2 * steps, KP, GROUP * KP), f32),
            pltpu.VMEM((flat_rows, 128), f32),
        ],
    )(m, first, second, cc, be, bf, up, idx, idxc, lops, cops, pool)
    potential, order = call(
        potential_kernel,
        (shape((part, atoms), bf16), shape((FOUR * 128, FOUR * 128), bf16)),
        [pltpu.VMEM((OCT * KP, leaf_dev), bf16), pltpu.VMEM((part, atoms), f32)],
    )(near, far, down, base, inside)

    axes = ("cells", "chan")
    if fits:
        parts = lax.all_to_all(grads, axes, 0, 0)
        spread_out = call(
            reduce_kernel,
            shape(laid, bf16),
            [pltpu.VMEM((laid[1] + 16, 128), f32), pltpu.VMEM((laid[1] + 16, 128), f32)],
            in_specs=[near_by, pl.BlockSpec(memory_space=pl.ANY), near_by],
        )(parts, potential, order)
        whole = lax.all_to_all(spread_out, axes, 0, 0)
    else:
        split = -(-flat_rows // devices) * devices
        pieces = jnp.pad(grads, ((0, split - flat_rows), (0, 0))).reshape(devices, -1, 128)
        parts = lax.all_to_all(pieces, axes, 0, 0)
        mine = jnp.sum(parts.astype(f32), axis=0).astype(bf16)
        whole = lax.all_gather(mine, axes).reshape(split, 128)[:flat_rows]
        whole = whole.reshape(flat_rows // FOUR, FOUR, 2, FOUR, 2, GROUP)
        whole = jnp.transpose(whole, (0, 3, 4, 1, 2, 5)).reshape(flat_rows, 128)
    grad_shape = shape((kcount, kcount, slots), f32)
    grad_leaf, grad_coarse = call(
        unpack_kernel, (grad_shape, grad_shape), [pltpu.VMEM((flat_rows, 128), f32)]
    )(whole)

    refined = call(
        mixing_kernel,
        shape((part, atoms), bf16),
        [pltpu.VMEM((mix.shape[0], atoms), f32)],
    )(lax.all_gather(potential, "chan", axis=0, tiled=True), mix_near, charges_near)
    return refined, grad_leaf, grad_coarse


def solution(mesh):
    placed = (
        P("chan", "cells"),
        P(None, "cells"),
        P("cells"),
        P(None, "cells"),
        P(None, "cells"),
        P(),
        P(),
        P(),
        P(),
        P(),
        P("chan", "cells"),
    )
    return jax.shard_map(
        local, mesh=mesh, in_specs=placed, out_specs=(P("chan", "cells"), P(), P()), check_vma=False
    )
```

```python
import functools

import jax
import jax.numpy as jnp
from jax import lax
from jax.experimental import pallas as pl
from jax.experimental.pallas import tpu as pltpu
from jax.sharding import PartitionSpec as P

KP = 32
GROUP = 8
KM = 24
CHUNK = 16
FOUR = 4
OCT = 8
MORE = 8
VMEM_BYTES = 24 * 1024 * 1024
f32 = jnp.float32
bf16 = jnp.bfloat16


def nt(a, b):
    return lax.dot_general(a, b, (((1,), (1,)), ((), ())), preferred_element_type=f32)


def nn(a, b):
    return jnp.dot(a, b, preferred_element_type=f32)


def member(leaf_row, leaf_dev):
    shape = (leaf_dev, leaf_row.shape[1])
    return jnp.where(lax.broadcasted_iota(jnp.int32, shape, 0) == leaf_row, 1.0, 0.0).astype(bf16)


def spread(base, values, scaled):
    wide = values.astype(f32)
    count = values.shape[0]
    for c in range(0, count, 2):
        pair = [base[0:KM, :] * wide[c + i : c + i + 1, :] for i in range(2)]
        scaled[c * KM : (c + 2) * KM, :] = jnp.concatenate(pair, axis=0).astype(bf16)
    scaled[count * KM :, :] = (base[KM : KM + 1, :] * wide).astype(bf16)


def lay_wide(rows, out):
    count = rows.shape[0] // (KM + 1)
    lanes = rows.shape[1]
    top = lax.broadcasted_iota(jnp.int32, (KP - KM, lanes), 0) == 0
    for c in range(count):
        last = jnp.where(top, rows[count * KM + c : count * KM + c + 1, :], 0.0)
        block = jnp.concatenate([rows[c * KM : (c + 1) * KM, :], last], axis=0)
        out[:, c * lanes : (c + 1) * lanes] = block.astype(bf16)


def fetch(pairs, sems):
    copies = [pltpu.make_async_copy(src, dst, sems.at[i]) for i, (src, dst) in enumerate(pairs)]
    for copy in copies:
        copy.start()
    return copies


def pooling(rows, cols):
    return jnp.where(
        lax.broadcasted_iota(jnp.int32, (rows, cols), 0) // OCT
        == lax.broadcasted_iota(jnp.int32, (rows, cols), 1),
        1.0,
        0.0,
    ).astype(bf16)


def by_octant(values):
    octant = lax.broadcasted_iota(jnp.int32, (1, values.shape[1]), 1) % OCT
    return jnp.concatenate(
        [values * jnp.where(octant == o, 1.0, 0.0).astype(values.dtype) for o in range(OCT)], axis=0
    )


def upward(ops, wide_ref, sums, pool):
    lanes = OCT * 128
    for part in range(wide_ref.shape[1] // lanes):
        spaced = by_octant(wide_ref[:, part * lanes : (part + 1) * lanes])
        sums[part * KP : (part + 1) * KP, :] = nn(ops, spaced).astype(bf16)
    return nn(sums[...], pool[...])


def tightened(rows):
    count = rows.shape[0] // KP
    whole = [rows[c * KP : c * KP + KM] for c in range(count)]
    last = [rows[c * KP + KM : c * KP + KM + 1] for c in range(count)]
    return jnp.concatenate(whole + last, axis=0).astype(bf16)


def moments_kernel(charges_hbm, basis_hbm, leaf_hbm, *rest):
    more = rest[:MORE]
    m_out, first_out, second_out, base_out, inside_out, pool_out, charges = rest[MORE : MORE + 7]
    held = rest[MORE + 7 : 2 * MORE + 7]
    basis, leaf, scaled, sems = rest[2 * MORE + 7 :]
    leaf_dev = m_out.shape[1]
    half = leaf_dev // 2
    cell = lax.axis_index("cells")
    copies = fetch(
        [(charges_hbm, charges), (basis_hbm, basis), (leaf_hbm, leaf), *zip(more, held)], sems
    )
    kcount = basis.shape[0]
    base_out[...] = jnp.zeros_like(base_out)
    pool_out[...] = pooling(*pool_out.shape)
    for copy in copies[:3]:
        copy.wait()
    base_out[0:kcount, :] = basis[...]
    inside_out[...] = member(leaf[...] - cell * leaf_dev, leaf_dev)
    spread(base_out, charges[...], scaled)
    m = nt(scaled[...], inside_out[...])
    m_out[...] = m.astype(bf16)
    rows = m.shape[0] // 2
    upper, lower = m[:rows], m[rows:]
    low_lane = lax.broadcasted_iota(jnp.int32, (rows, leaf_dev), 1) < half
    hi = jnp.where(low_lane, pltpu.roll(upper, half, 1), lower).astype(bf16)
    lo = jnp.where(low_lane, upper, pltpu.roll(lower, half, 1)).astype(bf16)
    odd = lax.rem(cell, 2)
    first_out[...] = jnp.where(odd == 1, hi, lo)
    second_out[...] = jnp.where(odd == 1, lo, hi)
    for copy in copies[3:]:
        copy.wait()


def slot_of(group, at):
    return at * GROUP + group


def slot_ops(ops, padded, turned, out):
    kcount, jcount, slots = ops.shape
    turned[...] = jnp.zeros_like(turned)
    padded[...] = jnp.zeros_like(padded)
    for k in range(kcount):
        padded[k, 0:jcount, 0:slots] = ops[k].astype(f32)
        turned[k, :, :] = padded[k].T[0:slots]
    for group in range(out.shape[0]):
        held = [turned[:, slot_of(group, at), :] for at in range(GROUP)]
        pieces = [a[:, 0:KM] for a in held] + [a[:, KM : KM + 1] for a in held]
        pieces.append(jnp.zeros((KP, GROUP * KP - GROUP * (KM + 1)), f32))
        out[group] = jnp.concatenate(pieces, axis=1).astype(bf16)


def prepare_kernel(
    up,
    down,
    lops,
    cops,
    ll,
    cl,
    m,
    pool,
    cc_out,
    up_out,
    down_out,
    back_out,
    lops_out,
    cops_out,
    idx,
    idxc,
    wide,
    stack,
    padded,
    turned,
    sums,
):
    leaf_dev = m.shape[1]
    half = leaf_dev // 2
    kcount = up.shape[0]
    coarse_dev, slots = cl.shape
    cell = lax.axis_index("cells")
    lay_wide(m[...].astype(f32), wide)
    stack[...] = jnp.zeros_like(stack)
    for k in range(kcount):
        stack[0, :, k, 0:kcount] = up[k].astype(f32)
        stack[1, :, k, 0:kcount] = down[k].astype(f32)

    def side_by_side(pieces):
        return jnp.concatenate(pieces, axis=1).astype(bf16)

    up_out[...] = side_by_side([stack[0, o, :, 0:KP] for o in range(OCT)])
    down_out[...] = side_by_side([stack[1, o, :, 0:KP] for o in range(OCT)])
    back_out[...] = side_by_side([stack[1, o].T[0:KP, :] for o in range(OCT)])
    cc_out[...] = tightened(upward(up_out[...], wide, sums, pool))

    slot_ops(lops, padded, turned, lops_out)
    slot_ops(cops, padded, turned, cops_out)
    rel = ll[...] - cell * leaf_dev
    place = jnp.where(rel < 0, rel + leaf_dev + half, jnp.where(rel < leaf_dev, rel, rel + half))
    idx[0:slots, :] = jnp.where(ll[...] < 0, -1, place)
    idx[slots:, :] = jnp.full_like(idx[slots:, :], -1)
    crel = cl[...] - cell * coarse_dev
    side = coarse_dev // 2
    cplace = jnp.where(crel < 0, crel + 128 + side, jnp.where(crel < coarse_dev, crel, crel + 128 - side))
    cplace = jnp.where(cl[...] < 0, -1, cplace).astype(f32).astype(bf16)
    copied = jnp.where(
        lax.broadcasted_iota(jnp.int32, (coarse_dev, 128), 0)
        == lax.broadcasted_iota(jnp.int32, (coarse_dev, 128), 1) % coarse_dev,
        1.0,
        0.0,
    ).astype(bf16)
    spot = lax.dot_general(cplace, copied, (((0,), (0,)), ((), ())), preferred_element_type=f32)
    spot = spot.astype(jnp.int32)
    start = lax.broadcasted_iota(jnp.int32, (slots, 128), 1) // coarse_dev * coarse_dev
    idxc[0:slots, :] = jnp.where(spot < 0, -1, spot + start)
    idxc[slots:, :] = jnp.full_like(idxc[slots:, :], -1)


def back_kernel(own, core, cross, other, mix, base, inside, pool, back_ops, be_out, bf_out, scaled, gathered, sums):
    part = own.shape[0]
    me = lax.axis_index("chan")
    gathered[pl.ds(me * part, part), :] = own[...]
    gathered[pl.ds((me ^ 1) * part, part), :] = core[...]
    gathered[pl.ds((me ^ 2) * part, part), :] = cross[...]
    gathered[pl.ds((me ^ 3) * part, part), :] = other[...]
    potential = nn(mix[pl.ds(me * part, part), :], gathered[...]).astype(bf16)
    spread(base, potential, scaled)
    lay_wide(nt(scaled[...], inside[...]), be_out)
    far = upward(back_ops[...], be_out, sums, pool).astype(bf16)
    for at in range(far.shape[0] // KP):
        bf_out[:, at * 128 : (at + 1) * 128] = far[at * KP : (at + 1) * KP, :]


def grads_kernel(
    m,
    first,
    second,
    cc,
    be,
    bf,
    up,
    idx,
    idxc,
    lops,
    cops,
    pool,
    near,
    far,
    g_out,
    src,
    srcc,
    wide,
    even,
    odd,
    even_c,
    odd_c,
    even_last,
    odd_last,
    even_c_last,
    odd_c_last,
    sums,
    blocks,
    flat,
    *,
    kcount,
):
    leaf_dev = m.shape[1]
    half = leaf_dev // 2
    window = 2 * leaf_dev
    channels = m.shape[0] // kcount
    steps = lops.shape[0]
    tight = even.shape[0]
    is_odd = lax.rem(lax.axis_index("cells"), 2) == 1

    src[:, 0:leaf_dev] = m[...]
    mid = first.shape[0]
    a, b = first[...].astype(f32), second[...].astype(f32)
    low, high = jnp.where(is_odd, b, a), jnp.where(is_odd, a, b)
    low_lane = lax.broadcasted_iota(jnp.int32, (mid, leaf_dev), 1) < half
    upper = jnp.where(low_lane, low, pltpu.roll(high, half, 1))
    lower = jnp.where(low_lane, pltpu.roll(low, half, 1), high)
    src[0:mid, leaf_dev:] = upper.astype(bf16)
    src[mid:, leaf_dev:] = lower.astype(bf16)
    place_of = lax.broadcasted_iota(jnp.int32, (window, 128), 0).astype(f32).astype(bf16)

    def chosen(ref, group, at):
        row = ref[pl.ds(slot_of(group, at), 1), :].astype(f32).astype(bf16)
        return jnp.where(place_of == row, jnp.ones((), bf16), jnp.zeros((), bf16))

    def picks(source, ref, group, held, last, chunk):
        count = source.shape[0] // kcount
        wide_by = 4 if count * KM < 128 else 2
        for first in range(0, GROUP, wide_by):
            both = jnp.concatenate([chosen(ref, group, first + i) for i in range(wide_by)], axis=1)
            for begin in range(0, count, chunk):
                end = begin + chunk
                end_row = end * KM if end < count else source.shape[0]
                picked = nn(source[begin * KM : end_row, :], both)
                for c in range(chunk):
                    rows = picked[c * KM : (c + 1) * KM]
                    lane = (begin + c) * 128
                    for i in range(0, wide_by, 2):
                        at = first + i
                        held[at * KM : (at + 2) * KM, lane : lane + 128] = jnp.concatenate(
                            [rows[:, i * 128 : (i + 1) * 128], rows[:, (i + 1) * 128 : (i + 2) * 128]], axis=0
                        ).astype(bf16)
            rows = picked[chunk * KM :]
            for i in range(wide_by):
                for c in range(count):
                    last[first + i : first + i + 1, c * 128 : (c + 1) * 128] = rows[c : c + 1, i * 128 : (i + 1) * 128]
        held[GROUP * KM :, :] = last[...].astype(bf16)

    def pick_leaves(group, held, last):
        picks(src, idx, group, held, last, CHUNK)

    def pick_parents(group, held_c, last_c):
        picks(srcc, idxc, group, held_c, last_c, srcc.shape[0] // kcount)

    def pick_group(group, held, last, held_c, last_c):
        pick_leaves(group, held, last)
        pick_parents(group, held_c, last_c)

    def gradients(group, held, held_c):
        blocks[group, :, 0:tight] = nt(be[...], held[...])
        blocks[steps + group, :, 0:tight] = nt(bf[...], held_c[...])

    def fields(group, held, held_c):
        near[...] += nn(lops[group][:, 0:tight], held[...])
        far[...] += nn(cops[group][:, 0:tight], held_c[...])

    for ref in (near, far, even_last, odd_last, even_c_last, odd_c_last):
        ref[...] = jnp.zeros_like(ref)
    evens, odds = (even, even_last, even_c, even_c_last), (odd, odd_last, odd_c, odd_c_last)
    pick_leaves(0, even, even_last)
    lay_wide(jnp.concatenate([upper, lower], axis=0), wide)
    srcc[:, 0:128] = cc[...]
    srcc[:, 128:] = tightened(upward(up[...], wide, sums, pool))
    pick_parents(0, even_c, even_c_last)

    def two_groups(i, carry):
        group = 2 * i + 1
        gradients(group - 1, even, even_c)
        pick_group(group, *odds)
        fields(group - 1, even, even_c)
        gradients(group, odd, odd_c)
        pick_group(group + 1, *evens)
        fields(group, odd, odd_c)
        return carry

    lax.fori_loop(0, steps // 2 - 1, two_groups, 0)
    pick_group(steps - 1, *odds)
    gradients(steps - 2, even, even_c)
    gradients(steps - 1, odd, odd_c)
    flat[...] = jnp.zeros_like(flat)
    main = GROUP * KM
    for turn in range(-(-kcount // FOUR)):
        several = jnp.concatenate([blocks[:, turn * FOUR + k, :] for k in range(FOUR)], axis=0)
        across = several.T
        for tile in range(GROUP // 2):
            at = 2 * tile
            body = jnp.concatenate([across[a * KM : (a + 1) * KM] for a in (at, at + 1)], axis=1)
            rest = jnp.concatenate([across[main + a : main + a + 1] for a in (at, at + 1)], axis=1)
            rows = pl.ds(turn * FOUR * kcount + tile, kcount, stride=FOUR)
            flat[rows, :] = jnp.concatenate([body, rest], axis=0)
    fields(steps - 2, even, even_c)
    fields(steps - 1, odd, odd_c)
    if len(g_out.shape) == 2:
        g_out[...] = flat[...].astype(bf16)
    else:
        for d in range(g_out.shape[0]):
            g_out[d] = flat[d * g_out.shape[1] : (d + 1) * g_out.shape[1], :].astype(bf16)


def potential_kernel(near, far, down, base, inside, out, order, field, total):
    leaf_dev = near.shape[1] // out.shape[0]
    lanes = OCT * 128
    copies = jnp.where(
        lax.broadcasted_iota(jnp.int32, (128, lanes), 1) // OCT
        == lax.broadcasted_iota(jnp.int32, (128, lanes), 0),
        1.0,
        0.0,
    ).astype(bf16)
    for at in range(far.shape[1] // 128):
        parent = nn(far[:, at * 128 : (at + 1) * 128].astype(bf16), copies).astype(bf16)
        child = nn(down[...], by_octant(parent))
        columns = slice(at * lanes, (at + 1) * lanes)
        expansion = (near[:, columns] + child).astype(bf16)
        for c in range(OCT):
            field[c * KP : (c + 1) * KP, :] = expansion[:, c * leaf_dev : (c + 1) * leaf_dev]
        for c in range(OCT):
            row = at * OCT + c
            per_atom = nn(field[c * KP : (c + 1) * KP, :], inside[...])
            total[row : row + 1, :] = jnp.sum(base[...] * per_atom, axis=0, keepdims=True)
    out[...] = total[...].astype(bf16)
    order[...] = turned_order()


def turned_order():
    size = FOUR * 128
    row = lax.broadcasted_iota(jnp.int32, (size, size), 0)
    k, level, group, at = row // 16 % FOUR, row // GROUP % 2, row % GROUP, row // 64
    wanted = k * 128 + level * 64 + slot_of(group, at)
    return jnp.where(lax.broadcasted_iota(jnp.int32, (size, size), 1) == wanted, 1.0, 0.0).astype(bf16)


def reduce_kernel(parts, after, order, out, total, laid):
    summed = parts[0].astype(f32)
    for d in range(1, parts.shape[0]):
        summed = summed + parts[d].astype(f32)
    total[0 : summed.shape[0], :] = summed
    count = summed.shape[0] // FOUR
    tiles = [total[pl.ds(tile, count, stride=FOUR), :] for tile in range(FOUR)]
    turned = nn(jnp.concatenate(tiles, axis=1).astype(bf16), order[...])
    for k in range(FOUR):
        laid[pl.ds(k, count, stride=FOUR), :] = turned[:, k * 128 : (k + 1) * 128]
    for d in range(out.shape[0]):
        out[d] = laid[0 : summed.shape[0], :].astype(bf16)


def unpack_kernel(whole, leaf_out, coarse_out, leaf, coarse, flat, sems):
    kcount, jcount, slots = leaf.shape
    if len(whole.shape) == 2:
        flat[...] = whole[...].astype(f32)
    else:
        for d in range(whole.shape[0]):
            flat[d * whole.shape[1] : (d + 1) * whole.shape[1], :] = whole[d].astype(f32)

    def row_of(k):
        return flat[pl.ds(k // FOUR * FOUR * jcount + k % FOUR, jcount, stride=FOUR), :]

    for k in range(kcount):
        leaf[k] = row_of(k)[:, 0:slots]
    first = pltpu.make_async_copy(leaf, leaf_out, sems.at[0])
    first.start()
    for k in range(kcount):
        coarse[k] = pltpu.roll(row_of(k), slots, 1)[:, 0:slots]
    second = pltpu.make_async_copy(coarse, coarse_out, sems.at[1])
    second.start()
    first.wait()
    second.wait()


def mixing_kernel(whole, mix, charges, out, mixed):
    part = out.shape[0]
    me = lax.axis_index("chan")
    mixed[...] = lax.dot_general(
        mix[...], whole[...], (((0,), (0,)), ((), ())), preferred_element_type=f32
    )
    out[...] = (charges[...].astype(f32) + mixed[pl.ds(me * part, part), :]).astype(bf16)


def call(kernel, outs, scratch, flops=10**8, moved=10**6, limit=VMEM_BYTES, **kw):
    return pl.pallas_call(
        kernel,
        out_shape=outs,
        scratch_shapes=scratch,
        compiler_params=pltpu.CompilerParams(vmem_limit_bytes=limit),
        cost_estimate=pl.CostEstimate(flops=flops, bytes_accessed=moved, transcendentals=0),
        **kw,
    )


def from_chan(block):
    count = lax.axis_size("chan")

    def swap(part, d):
        return lax.ppermute(part, "chan", [(i, i ^ d) for i in range(count)])

    cross = swap(block, 2)
    return [swap(block, 1), cross, swap(cross, 1)]


def local(
    charges, basis, atom_leaf, leaf_lists, coarse_lists, up_ops, down_ops, leaf_ops, coarse_ops, mix, cotangent
):
    part, atoms = charges.shape
    kcount = basis.shape[0]
    slots, leaf_dev = leaf_lists.shape
    rows = part * kcount
    coarse_rows = rows // OCT
    steps = slots // GROUP
    cells = lax.axis_size("cells")
    devices = cells * lax.axis_size("chan")
    leaf = atom_leaf.reshape(1, atoms)
    shape = jax.ShapeDtypeStruct
    far_off = pl.BlockSpec(memory_space=pltpu.HBM)
    near_by = pl.BlockSpec(memory_space=pltpu.VMEM)
    like = lambda a: pltpu.VMEM(a.shape, a.dtype)
    stay = lambda *arrays: [pltpu.with_memory_space_constraint(a, pltpu.HBM) for a in arrays]
    wide = part * leaf_dev

    held = (
        cotangent,
        mix,
        jnp.swapaxes(up_ops, 0, 1),
        jnp.swapaxes(down_ops, 0, 1),
        leaf_ops,
        coarse_ops,
        leaf_lists,
        coarse_lists.T,
    )
    m, first, second, base, inside, pool, charges_near, *held = call(
        moments_kernel,
        (
            shape((rows, leaf_dev), bf16),
            shape((rows // 2, leaf_dev), bf16),
            shape((rows // 2, leaf_dev), bf16),
            shape((KP, atoms), f32),
            shape((leaf_dev, atoms), bf16),
            shape((OCT * 128, 128), bf16),
            shape(charges.shape, bf16),
            *[shape(a.shape, a.dtype) for a in held],
        ),
        [like(basis), like(leaf), pltpu.VMEM((rows, atoms), bf16), pltpu.SemaphoreType.DMA((3 + MORE,))],
        in_specs=[far_off] * (3 + MORE),
    )(*stay(charges, basis, leaf, *held))
    inner = [(i, i + 1) for i in range(1, cells - 1, 2)]
    outer = [(i, i + 1) for i in range(0, cells - 1, 2)]
    first = lax.ppermute(first, "cells", inner + [(b, a) for a, b in inner])
    second = lax.ppermute(second, "cells", outer + [(b, a) for a, b in outer])
    own, mix_near, *prepared = held
    cot = from_chan(own)

    wide_ops = shape((KP, OCT * KP), bf16)
    group_ops = shape((steps, KP, GROUP * KP), bf16)
    cc, up, down, back_ops, lops, cops, idx, idxc = call(
        prepare_kernel,
        (
            shape((coarse_rows, 128), bf16),
            wide_ops,
            wide_ops,
            wide_ops,
            group_ops,
            group_ops,
            shape((slots + 8, 128), jnp.int32),
            shape((slots + 8, 128), jnp.int32),
        ),
        [
            pltpu.VMEM((KP, wide), bf16),
            pltpu.VMEM((2, OCT, KP, 128), f32),
            pltpu.VMEM((kcount, KP, 128), f32),
            pltpu.VMEM((KP, slots, KP), f32),
            pltpu.VMEM((128, OCT * 128), bf16),
        ],
        flops=10**8,
    )(*prepared, m, pool)
    be, bf = call(
        back_kernel,
        (shape((KP, wide), bf16), shape((KP, wide // OCT), bf16)),
        [
            pltpu.VMEM((rows, atoms), bf16),
            pltpu.VMEM((mix.shape[0], atoms), bf16),
            pltpu.VMEM((128, OCT * 128), bf16),
        ],
    )(own, *cot, mix_near, base, inside, pool, back_ops)

    flat_rows = -(-(-(-kcount // FOUR) * FOUR * kcount) // 256) * 256
    fits = flat_rows % (8 * devices) == 0
    laid = (devices, flat_rows // devices, 128) if fits else (flat_rows, 128)
    near, far, grads = call(
        functools.partial(grads_kernel, kcount=kcount),
        (shape((KP, wide), f32), shape((KP, wide // OCT), f32), shape(laid, bf16)),
        [
            pltpu.VMEM((rows, 2 * leaf_dev), bf16),
            pltpu.VMEM((coarse_rows, 256), bf16),
            pltpu.VMEM((KP, wide), bf16),
            pltpu.VMEM((GROUP * KM + 16, wide), bf16),
            pltpu.VMEM((GROUP * KM + 16, wide), bf16),
            pltpu.VMEM((GROUP * KM + 16, wide // OCT), bf16),
            pltpu.VMEM((GROUP * KM + 16, wide // OCT), bf16),
            pltpu.VMEM((16, wide), f32),
            pltpu.VMEM((16, wide), f32),
            pltpu.VMEM((16, wide // OCT), f32),
            pltpu.VMEM((16, wide // OCT), f32),
            pltpu.VMEM((128, OCT * 128), bf16),
            pltpu.VMEM((2 * steps, KP, GROUP * KP), f32),
            pltpu.VMEM((flat_rows, 128), f32),
        ],
    )(m, first, second, cc, be, bf, up, idx, idxc, lops, cops, pool)
    potential, order = call(
        potential_kernel,
        (shape((part, atoms), bf16), shape((FOUR * 128, FOUR * 128), bf16)),
        [pltpu.VMEM((OCT * KP, leaf_dev), bf16), pltpu.VMEM((part, atoms), f32)],
    )(near, far, down, base, inside)

    axes = ("cells", "chan")
    if fits:
        parts = lax.all_to_all(grads, axes, 0, 0)
        spread_out = call(
            reduce_kernel,
            shape(laid, bf16),
            [pltpu.VMEM((laid[1] + 16, 128), f32), pltpu.VMEM((laid[1] + 16, 128), f32)],
            in_specs=[near_by, pl.BlockSpec(memory_space=pl.ANY), near_by],
        )(parts, potential, order)
        whole = lax.all_to_all(spread_out, axes, 0, 0)
    else:
        split = -(-flat_rows // devices) * devices
        pieces = jnp.pad(grads, ((0, split - flat_rows), (0, 0))).reshape(devices, -1, 128)
        parts = lax.all_to_all(pieces, axes, 0, 0)
        mine = jnp.sum(parts.astype(f32), axis=0).astype(bf16)
        whole = lax.all_gather(mine, axes).reshape(split, 128)[:flat_rows]
        whole = whole.reshape(flat_rows // FOUR, FOUR, 2, FOUR, 2, GROUP)
        whole = jnp.transpose(whole, (0, 3, 4, 1, 2, 5)).reshape(flat_rows, 128)
    grad_shape = shape((kcount, kcount, slots), f32)
    grad_leaf, grad_coarse = call(
        unpack_kernel,
        (grad_shape, grad_shape),
        [
            pltpu.VMEM(grad_shape.shape, f32),
            pltpu.VMEM(grad_shape.shape, f32),
            pltpu.VMEM((flat_rows, 128), f32),
            pltpu.SemaphoreType.DMA((2,)),
        ],
        out_specs=[far_off, far_off],
    )(whole)

    refined = call(
        mixing_kernel,
        shape((part, atoms), bf16),
        [pltpu.VMEM((mix.shape[0], atoms), f32)],
    )(lax.all_gather(potential, "chan", axis=0, tiled=True), mix_near, charges_near)
    return refined, grad_leaf, grad_coarse


def solution(mesh):
    placed = (
        P("chan", "cells"),
        P(None, "cells"),
        P("cells"),
        P(None, "cells"),
        P(None, "cells"),
        P(),
        P(),
        P(),
        P(),
        P(),
        P("chan", "cells"),
    )
    return jax.shard_map(
        local, mesh=mesh, in_specs=placed, out_specs=(P("chan", "cells"), P(), P()), check_vma=False
    )
```
